128 devices in a mesh: layer: 16 (over x, y), attn: 8 (over z, core).
Axes of the slice: x: 4, y: 4, z: 4, core: 2. Of those that a mesh axis runs over, the one named last changes fastest.
Arguments:
- tokens: bfloat16 [8192, 8192], P('layer', 'attn'), may hold values from -6 to 6
- norm_gain: float32 [8192], replicated, may hold values from 0.1 to 1.9
- qkv_weight: bfloat16 [8192, 10240], P('layer', 'attn')
- doc_ids: int32 [8192], replicated, may hold values from 0 to 7, as said below
- block_server: int32 [128], replicated, may hold values from 0 to 15, as said below
Outputs:
- served: bfloat16 [8192, 8192], P('layer', 'attn')
The draws below stay inside these ranges and needn't reach their ends.
Inputs may be any that keep to these rules, and one draw needn't show every extreme that they name: `doc_ids`: each document is a run of consecutive tokens, numbers never fall along the pack, every one of the 8 documents has at least one token, each has at most 2048 tokens and one has exactly 2048. `block_server`: the 8 stretches of one index of layer (stretches i * 8 to (i + 1) * 8 - 1) go to 8 different servers, and every server receives exactly 8 stretches. The plan is built from doc_ids to even out the causal work over servers: a stretch's cost is the number of tokens from its document's first token to its own last token, and each index of layer in turn gives its costliest stretches to the least loaded of its servers.
All inputs are finite; a program needn't handle non-finite values.
Results may differ from the reference program's by a relative error of at most 0.013.
The reference program's roundings to bfloat16 on the way count: a program that leaves them out, or rounds other values in their place, can miss the bound.
Values may be sent and summed in bfloat16 or wider, within the bound.
A program may use at most 128 MiB of HBM per device.

```python
import math
import jax
import jax.numpy as jnp
from jax import lax

D = 8192
HEAD_DIM = 128
GROUP = 8
BLOCK = 64
KV_HEADS = 8
TOKENS = 8192
BLK_DEV = 8
N_BLOCKS = 128
DOCS = 8
DOC_MOST = 2048
N_LAYER = 16


def draw_qkv_weight(key, part):
    key = jax.random.fold_in(key, 5)
    width = KV_HEADS * (GROUP + 2) * HEAD_DIM
    base = jax.random.normal(key, (D, width), jnp.float32)
    return (base * float(D) ** (-0.5)).astype(jnp.bfloat16)


def doc_ends(key):
    shared = jax.random.fold_in(key, 101)
    move_key, order_key = jax.random.split(shared, 2)
    others = DOCS - 1
    rest = TOKENS - DOC_MOST
    base = rest // others
    extra = rest - base * others
    moves = jax.random.randint(move_key, (others,), 0, base, dtype=jnp.int32)
    index = jnp.arange(others, dtype=jnp.int32)
    sign = jnp.where(index % 2 == 0, -1, 1).astype(jnp.int32)
    amount = moves[index - index % 2]
    lonely = (index == others - 1) & (others % 2 == 1)
    amount = jnp.where(lonely, 0, amount).astype(jnp.int32)
    lengths_rest = base + sign * amount + jnp.where(index == others - 1, extra, 0).astype(jnp.int32)
    lengths = jnp.concatenate([jnp.full((1,), DOC_MOST, jnp.int32), lengths_rest.astype(jnp.int32)])
    lengths = lengths[jax.random.permutation(order_key, DOCS)]
    return jnp.cumsum(lengths).astype(jnp.int32)


def draw_doc_ids(key, part):
    ends = doc_ends(key)
    positions = jnp.arange(TOKENS, dtype=jnp.int32)
    return jnp.sum((positions[:, None] >= ends[None, :]).astype(jnp.int32), axis=1).astype(jnp.int32)


def draw_block_server(key, part):
    ends = doc_ends(key)
    key = jax.random.fold_in(key, 11)
    first_key, third_key = jax.random.split(key, 2)
    starts = jnp.concatenate([jnp.zeros((1,), jnp.int32), ends[:-1]])
    stretch_first = jnp.arange(N_BLOCKS, dtype=jnp.int32) * BLOCK
    stretch_doc = jnp.sum((stretch_first[:, None] >= ends[None, :]).astype(jnp.int32), axis=1)
    costs = (stretch_first + BLOCK - starts[stretch_doc]).astype(jnp.int32).reshape(N_LAYER, BLK_DEV)
    offsets = jax.random.permutation(first_key, N_LAYER)[:BLK_DEV].astype(jnp.int32)
    relabel = jax.random.permutation(third_key, N_LAYER).astype(jnp.int32)
    slots = jnp.arange(BLK_DEV, dtype=jnp.int32)

    def assign(loads, source):
        servers_here = relabel[(source + offsets) % N_LAYER]
        cost_here = lax.dynamic_index_in_dim(costs, source, 0, keepdims=False)
        stretch_rank = jnp.argsort(-(cost_here * BLK_DEV + (BLK_DEV - 1 - slots)), stable=True)
        server_rank = jnp.argsort(loads[servers_here] * N_LAYER + servers_here, stable=True)
        chosen = servers_here[server_rank]
        targets = jnp.zeros((BLK_DEV,), jnp.int32).at[stretch_rank].set(chosen)
        loads = loads.at[chosen].add(cost_here[stretch_rank])
        return (loads, targets)
    unused_loads, plan = lax.scan(assign, jnp.zeros((N_LAYER,), jnp.int32), jnp.arange(N_LAYER, dtype=jnp.int32))
    return plan.reshape(-1).astype(jnp.int32)


def block_scale(own_key, shape, shards, low, top_value):
    loudness, own = 1.0, jax.random.fold_in(own_key, 6)
    for axis_at, shards_of in shards:
        steps = jnp.exp(jax.random.uniform(jax.random.fold_in(own, axis_at), (shards_of,), jnp.float32, low / len(shards), top_value / len(shards)))
        loudness = loudness * jnp.repeat(steps, shape[axis_at] // shards_of).reshape([-1 if axis == axis_at else 1 for axis in range(len(shape))])
    return loudness


def gaussian(key, extent, deviation, reach, shards=(), held_as=jnp.bfloat16):
    array = jax.random.normal(key, extent, jnp.float32) * deviation
    if len(shards) > 0:
        array = block_scale(key, extent, shards, -0.22, 0.18) * array
    return jnp.clip(array, min=-reach, max=reach).astype(held_as)


def setup_inputs(seed: int = 0) -> dict:
    keys = jax.random.split(jax.random.key(seed), 6)
    tokens = gaussian(keys[0], (TOKENS, D), 1.0, 6.0, ((0, 16), (1, 8)))
    norm_gain = jnp.clip(1.0 + 0.18 * jax.random.normal(keys[1], (D,), jnp.float32), 0.1, 1.9)
    qkv_weight = draw_qkv_weight(jax.random.fold_in(keys[5], 71), 0)
    doc_ids = draw_doc_ids(jax.random.fold_in(keys[5], 71), 0)
    block_server = draw_block_server(jax.random.fold_in(keys[5], 71), 0)
    return dict(tokens=tokens, norm_gain=norm_gain, qkv_weight=qkv_weight, doc_ids=doc_ids, block_server=block_server)


EPSILON = 1e-05
KEY_SPAN = 512
NEG_FLOOR = -1e+30

def norm_rows(wide_rows, norm_gain):
    values_f = wide_rows.astype(jnp.float32)
    moment = lax.optimization_barrier(jnp.mean(values_f * values_f, axis=-1, keepdims=True))
    return (values_f * lax.rsqrt(moment + EPSILON) * norm_gain).astype(jnp.bfloat16)

def attend_block(query_block, block_first, all_keys, all_values, doc_ids):
    block_len, query_cols = query_block.shape
    head_size = all_keys.shape[1]
    heads = query_cols // head_size
    total_len = all_keys.shape[0]
    key_block = math.gcd(KEY_SPAN, total_len)
    queries = query_block.reshape(block_len, heads, head_size).astype(jnp.float32)
    row_first = (block_first * block_len).astype(jnp.int32)
    query_pos = row_first + jnp.arange(block_len, dtype=jnp.int32)
    query_doc = lax.dynamic_slice_in_dim(doc_ids, row_first, block_len, 0)
    doc_first = jnp.sum((doc_ids < query_doc[0]).astype(jnp.int32)).astype(jnp.int32)
    lower = (doc_first // key_block).astype(jnp.int32)
    upper = ((row_first + block_len + key_block - 1) // key_block).astype(jnp.int32)
    scaling = 1.0 / math.sqrt(head_size)

    def visit(step, running):
        run_max, sums, output = running
        key_first = (step * key_block).astype(jnp.int32)
        key_rows = lax.dynamic_slice_in_dim(all_keys, key_first, key_block, 0).astype(jnp.float32)
        value_rows = lax.dynamic_slice_in_dim(all_values, key_first, key_block, 0).astype(jnp.float32)
        key_pos = key_first + jnp.arange(key_block, dtype=jnp.int32)
        key_doc = lax.dynamic_slice_in_dim(doc_ids, key_first, key_block, 0)
        scores = jnp.einsum('thd,sd->hts', queries, key_rows, precision=lax.Precision.HIGHEST) * scaling
        allowed = ((key_pos[None, :] <= query_pos[:, None]) & (key_doc[None, :] == query_doc[:, None]))[None]
        masked = jnp.where(allowed, scores, NEG_FLOOR)
        new_max = jnp.maximum(run_max, lax.optimization_barrier(jnp.max(masked, axis=-1)))
        rescale = jnp.exp(run_max - new_max)
        probs = jnp.where(allowed, jnp.exp(scores - new_max[..., None]), 0.0)
        rounded = lax.optimization_barrier(probs.astype(jnp.bfloat16)).astype(jnp.float32)
        output = output * rescale[..., None] + jnp.einsum('hts,sd->htd', rounded, value_rows, precision=lax.Precision.HIGHEST)
        sums = sums * rescale + lax.optimization_barrier(jnp.sum(probs, axis=-1))
        return (new_max, sums, output)
    start_state = (jnp.full((heads, block_len), NEG_FLOOR, jnp.float32), jnp.zeros((heads, block_len), jnp.float32), jnp.zeros((heads, block_len, head_size), jnp.float32))
    run_max, sums, output = lax.fori_loop(lower, upper, visit, start_state)
    output = output / sums[..., None]
    return output.transpose(1, 0, 2).reshape(block_len, query_cols).astype(jnp.bfloat16)

def reference(tokens, norm_gain, qkv_weight, doc_ids, block_server):
    normed = norm_rows(tokens, norm_gain)
    projected = jnp.dot(normed, qkv_weight, preferred_element_type=jnp.float32).astype(jnp.bfloat16)
    total_len = tokens.shape[0]
    group_cols = (GROUP + 2) * HEAD_DIM
    kv_groups = qkv_weight.shape[1] // group_cols
    grouped = projected.reshape(total_len, kv_groups, GROUP + 2, HEAD_DIM)
    block_ids = jnp.arange(N_BLOCKS, dtype=jnp.int32)

    def one_group(group_id):
        slab = lax.dynamic_index_in_dim(grouped, group_id, 1, keepdims=False)
        queries = slab[:, :GROUP].reshape(N_BLOCKS, BLOCK, GROUP * HEAD_DIM)
        keys_all = slab[:, GROUP]
        values_all = slab[:, GROUP + 1]

        def one_block(pair_items):
            return attend_block(pair_items[0], pair_items[1], keys_all, values_all, doc_ids)
        return lax.map(one_block, (queries, block_ids))
    attended = lax.map(one_group, jnp.arange(kv_groups, dtype=jnp.int32))
    order = jnp.argsort(block_server.astype(jnp.int32) * N_BLOCKS + block_ids, stable=True)
    served = jnp.take(attended, order, axis=1)
    return served.transpose(1, 2, 0, 3).reshape(total_len, kv_groups * GROUP * HEAD_DIM)
```

```python
import math

import jax
import jax.numpy as jnp
from jax import lax
from jax.experimental import pallas as pl
from jax.experimental.pallas import tpu as pltpu
from jax.sharding import PartitionSpec as P

MESH = pl.DeviceIdType.MESH
HEAD_DIM = 128
GROUP = 8
BLOCK = 64
STEP = 512
BACK = 4
RING = 4
LAYERS = 16
ATTN = 8
ROWS = 512
COLS = 1024
WIDE = 256
CHUNKS = 5
HALF = 256

EPSILON = 1e-05
LOG2E = math.log2(math.e)
NEG_FLOOR = -1e30 * LOG2E
MASKED = -3e38
SCALING = LOG2E / math.sqrt(HEAD_DIM)


def remote(src, dst, send_sem, recv_sem, **device):
    return pltpu.make_async_remote_copy(
        src_ref=src,
        dst_ref=dst,
        send_sem=send_sem,
        recv_sem=recv_sem,
        device_id=device,
        device_id_type=MESH,
    )


def fused_kernel(
    tok_ref,
    gain_ref,
    w_ref,
    doc_ref,
    plan_ref,
    out_ref,
    mine,
    normed,
    weights,
    keys,
    values,
    bias,
    pick,
    keep,
    attended,
    slots,
    landed,
    acc,
    moments,
    own_sem,
    pair_send,
    pair_recv,
    w_send,
    w_recv,
    core_send,
    core_recv,
    share_send,
    share_recv,
    t_send,
    t_recv,
    m_send,
    m_recv,
    kv_send,
    kv_recv,
    s_send,
    s_recv,
):
    layer = lax.axis_index("layer")
    attn = lax.axis_index("attn")
    x, y = layer // RING, layer % RING
    z, core = attn // 2, attn % 2
    side = y // 2
    partner = x * RING + 3 - y
    inner = x * RING + y + 1 - 2 * (y % 2)
    unit = ((y + 1) // 2) % 2
    same = 1 - (core - side) * (core - side)
    home, away = core == side, core != side
    rows_at = same * layer + (1 - same) * partner
    sibling = attn + 1 - 2 * core
    group = 2 * z + side

    def holder(row):
        row = row % LAYERS
        across, along = row // RING, row % RING
        inside = 1 - (along // 2 - side) * (along // 2 - side)
        along = inside * along + (1 - inside) * (3 - along)
        core_there = inside * side + (1 - inside) * (1 - side)
        return {"layer": across * RING + along, "attn": 2 * z + core_there}

    def across_x(step):
        return {"layer": ((x + step) % RING) * RING + y}

    def along_z(step):
        return {"attn": (attn + 2 * step) % ATTN}

    shift = (1, -1)
    sent = {"all": [], "home": [], "away": [], 0: [], 1: []}
    condition = {"home": home, "away": away, 0: core == 0, 1: core == 1}

    def go(copies, who="all"):
        if who == "all":
            for copy in copies:
                copy.start()
        else:

            @pl.when(condition[who])
            def _():
                for copy in copies:
                    copy.start()

        sent[who].extend(copies)

    def arrive(copies, who="all"):
        if who == "all":
            for copy in copies:
                copy.wait_recv()
        else:

            @pl.when(condition[who])
            def _():
                for copy in copies:
                    copy.wait_recv()

    barrier = pltpu.get_barrier_semaphore()
    for step in range(1, LAYERS):
        for at in (attn, sibling):
            pl.semaphore_signal(
                barrier,
                inc=1,
                device_id={"layer": (layer + step) % LAYERS, "attn": at},
                device_id_type=MESH,
            )
    for step in range(1, ATTN):
        pl.semaphore_signal(
            barrier, inc=1, device_id={"attn": (attn + step) % ATTN}, device_id_type=MESH
        )
    pl.semaphore_wait(barrier, 2 * (LAYERS - 1) + ATTN - 1)

    def columns(chunk):
        first = GROUP * HEAD_DIM if chunk == 0 else (chunk - 1) * WIDE
        return pl.ds(first, WIDE)

    def w_pair(chunk):
        def share(half):
            rows = pl.ds(pl.multiple_of(half * HALF, HALF), HALF)
            return w_ref.at[rows, columns(chunk)], weights.at[chunk, half, x, unit, side]

        src, dst = share(1 - core)
        go(
            [
                remote(
                    src,
                    dst,
                    pair_send.at[chunk, 0],
                    pair_recv.at[chunk, 1 - same],
                    layer=rows_at,
                    attn=sibling,
                )
            ]
        )
        src, dst = share(core)
        go(
            [
                remote(
                    src,
                    dst,
                    pair_send.at[chunk, 1],
                    pair_recv.at[chunk, 1],
                    layer=partner,
                    attn=attn,
                )
            ],
            "away",
        )
        own = pltpu.make_async_copy(src, dst, own_sem.at[chunk])

        @pl.when(home)
        def _():
            own.start()

        return own

    def w_legs(chunk):
        ring = [across_x(shift[way]) for way in range(2)]
        cols = [x, (x - 1) % RING, (x + 1) % RING, (x + 2) % RING]

        def leg(ref, index, device):
            return remote(
                ref, ref, w_send.at[chunk, index], w_recv.at[chunk, index], **device
            )

        inside = {"layer": inner}
        first = {0: {}, 1: {}}
        units = [weights.at[chunk, 0, cols[k], unit] for k in range(4)]
        first[0]["near"] = [leg(units[0], way, ring[way]) for way in range(2)]
        first[0]["far"] = [
            leg(weights.at[chunk, 0, cols[1 + way], unit, way], 3 + way, ring[way])
            for way in range(2)
        ]
        first[0]["inner"] = [leg(units[k], (2, 5, 6, 7)[k], inside) for k in range(4)]
        first[1]["inner"] = [leg(weights.at[chunk, 1, x, unit], 0, inside)]
        first[1]["near"] = [leg(weights.at[chunk, 1, x], 1 + way, ring[way]) for way in range(2)]
        first[1]["far"] = [
            leg(weights.at[chunk, 1, cols[1 + way], way], 3 + way, ring[way]) for way in range(2)
        ]
        first["core"] = [
            remote(
                weights.at[chunk, core, cols[k]],
                weights.at[chunk, core, cols[k]],
                core_send.at[chunk, k],
                core_recv.at[chunk, k],
                attn=sibling,
            )
            for k in range(4)
        ]
        return first

    own_copies = {}
    legs = {}

    def w_start(chunk):
        own_copies[chunk] = w_pair(chunk)

    def w_one(chunk):
        legs[chunk] = w_legs(chunk)
        got = legs[chunk]
        place = weights.at[chunk, core, x, unit, side]
        from_core = remote(
            place, place, pair_send.at[chunk, 0], pair_recv.at[chunk, 0], attn=sibling
        )
        from_pair = remote(
            place, place, pair_send.at[chunk, 0], pair_recv.at[chunk, 1], layer=partner
        )

        @pl.when(home)
        def _():
            own_copies[chunk].wait()

        arrive([from_core], "away")
        arrive([from_pair])
        go([got[0]["near"][0], got[0]["near"][1], got[0]["inner"][0]], 0)
        go(got[1]["inner"], 1)

    def w_two(chunk):
        got = legs[chunk]
        for way in range(2):
            arrive([got[0]["near"][way]], 0)
            go([got[0]["far"][way], got[0]["inner"][1 + way]], 0)
        arrive(got[1]["inner"], 1)
        go(got[1]["near"] + [], 1)
        go([got["core"][0]], 1)

    def w_three(chunk):
        got = legs[chunk]
        arrive(got[0]["far"], 0)
        go([got[0]["inner"][3]], 0)
        for k in range(3):
            arrive([got[0]["inner"][k]], 0)
            go([got["core"][k]], 0)
        for way in range(2):
            arrive([got[1]["near"][way]], 1)
            go([got[1]["far"][way], got["core"][1 + way]], 1)

    def w_four(chunk):
        got = legs[chunk]
        arrive([got[0]["inner"][3]], 0)
        arrive(got[1]["far"], 1)
        go([got["core"][3]])

    def w_wait(chunk):
        arrive(legs[chunk]["core"])

    w_start(0)
    w_start(1)

    tokens = tok_ref[...].astype(jnp.float32)
    own_sum = jnp.sum(tokens * tokens, axis=1, keepdims=True)
    moments[attn] = jnp.transpose(jnp.broadcast_to(own_sum, (ROWS, 128)))[:8]
    m_copies = [
        remote(
            moments.at[attn],
            moments.at[attn],
            m_send.at[step - 1],
            m_recv.at[step - 1],
            attn=(attn + step) % ATTN,
        )
        for step in range(1, ATTN)
    ]
    go(m_copies)
    acc[...] = jnp.zeros_like(acc)
    arrive(m_copies)
    total = moments[0]
    for at in range(1, ATTN):
        total = total + moments[at]
    total = jnp.transpose(jnp.broadcast_to(total[:1], (128, ROWS)))[:, :1]
    scale = lax.rsqrt(total * (1.0 / (ATTN * COLS)) + EPSILON)
    gain = gain_ref[pl.ds(pl.multiple_of(attn * COLS, COLS), COLS)].reshape(1, COLS)
    mine[...] = (tok_ref[...].astype(jnp.float32) * scale * gain).astype(jnp.bfloat16)

    def share_copy(half, index, **device):
        rows = pl.ds(half * HALF, HALF)
        return remote(
            mine.at[rows],
            normed.at[attn, rows],
            share_send.at[index, half],
            share_recv.at[core, half],
            **device,
        )

    for half in range(2):
        go([share_copy(half, 0, layer=partner, attn=group)])
        go([share_copy(half, 1, attn=sibling)], "away")

    @pl.when(home)
    def _():
        normed[attn] = mine[...]

    def share_wait(which, half):
        rows = normed.at[2 * z + which, pl.ds(half * HALF, HALF)]
        return remote(
            rows, rows, share_send.at[0, half], share_recv.at[which, half], layer=partner
        )

    def z_rows(block, half):
        return normed.at[pl.ds(2 * (block % RING), 2), pl.ds(half * HALF, HALF)]

    def z_copy(ref, index, way):
        return remote(ref, ref, t_send.at[index], t_recv.at[index], **along_z(shift[way]))

    z_near = {
        (half, way): z_copy(z_rows(z, half), 2 * half + way, way)
        for half in range(2)
        for way in range(2)
    }
    z_far = [z_copy(z_rows(z - shift[way], way), 4 + way, way) for way in range(2)]
    share_pair = {half: [share_wait(0, half), share_wait(1, half)] for half in range(2)}
    share_core = {half: [share_wait(1 - core, half)] for half in range(2)}

    def z_start(who, half):
        arrive(share_core[half] if who == "home" else share_pair[half], who)
        go([z_near[half, 0], z_near[half, 1]], who)

    def z_forward(who, way):
        arrive([z_near[way, way]], who)
        go([z_far[way]], who)

    z_start("home", 0)
    z_start("home", 1)
    w_start(2)
    w_one(0)
    w_two(0)
    w_one(1)

    def one_hot(table, first, second, at):
        rows = table.shape[0]
        row_at = lax.broadcasted_iota(jnp.int32, (rows, 128), 0)
        col_at = lax.broadcasted_iota(jnp.int32, (rows, 128), 1)
        wanted = jnp.where(col_at < BLOCK, first, second)
        hit = (row_at // BLOCK == wanted) & (row_at % BLOCK == col_at % BLOCK)
        table[:, at * 128 : (at + 1) * 128] = jnp.where(hit, 1.0, 0.0).astype(jnp.bfloat16)

    blocks = ROWS // BLOCK
    for at in range(blocks // 2):
        first = rows_at * blocks + 2 * at
        one_hot(pick, plan_ref[first], plan_ref[first + 1], at)

    z_start("away", 0)
    w_three(0)
    w_two(1)

    places = []
    count = 0
    for source in range(LAYERS):
        present = 0
        for at in range(blocks):
            present = present + jnp.where(plan_ref[source * blocks + at] == layer, 1, 0)
        places.append(jnp.where(present == 1, count, -1))
        count = count + present
    for at in range(LAYERS // 2):
        one_hot(keep, places[2 * at], places[2 * at + 1], at)

    def doc_row(source):
        row = doc_ref[pl.ds(pl.multiple_of(source * STEP, STEP), STEP)]
        return row.reshape(1, STEP).astype(jnp.float32)

    row_doc = jnp.transpose(jnp.broadcast_to(doc_row(rows_at), (128, STEP)))[:, :1]
    row_at = lax.broadcasted_iota(jnp.int32, (ROWS, STEP), 0)
    key_at = lax.broadcasted_iota(jnp.int32, (ROWS, STEP), 1)
    for j in range(BACK + 1):
        source = rows_at - BACK + j
        key_doc = doc_row((source + LAYERS) % LAYERS)
        allowed = jnp.where(source < 0, -1.0, key_doc) == row_doc
        if j == BACK:
            allowed = allowed & (key_at <= row_at)
        bias[j] = jnp.where(allowed, 0.0, MASKED)

    def project(chunks, first, count):
        low, many = chunks

        @pl.loop(0, 2 * count * many)
        def _(at):
            place = at % 2
            block = (z + first + 2 * ((at // 2) % count)) % RING
            chunk = low + at // (2 * count)
            parts = [
                weights[chunk, half, block, spot, place]
                for spot in (place, 1 - place)
                for half in range(2)
            ]
            acc[chunk] += jnp.dot(
                normed[2 * block + place],
                jnp.concatenate(parts, axis=0),
                preferred_element_type=jnp.float32,
            )

    w_start(3)
    w_one(2)
    z_start("away", 1)
    w_four(0)
    z_forward("home", 0)
    z_forward("home", 1)
    w_three(1)
    w_two(2)
    w_start(4)
    w_one(3)
    w_wait(0)
    project((0, 1), 0, 1)
    w_four(1)
    w_three(2)
    w_two(3)
    w_one(4)
    w_wait(1)
    project((1, 1), 0, 1)
    z_forward("away", 0)
    z_forward("away", 1)
    w_four(2)
    w_three(3)
    w_two(4)
    for at in ((0, 1), (1, 0)):
        arrive([z_near[at]])
    project((0, 2), 1, 2)
    w_four(3)
    w_three(4)
    w_wait(2)
    project((2, 1), 0, 1)
    project((2, 1), 1, 2)
    w_wait(3)
    project((3, 1), 0, 1)
    project((3, 1), 1, 2)
    w_four(4)
    arrive(z_far)

    project((0, 1), 2, 1)
    keys[BACK] = jnp.transpose(acc[0, :, :HEAD_DIM]).astype(jnp.bfloat16)
    values[BACK] = acc[0, :, HEAD_DIM:].astype(jnp.bfloat16)
    kv_copies = [
        remote(
            table.at[BACK],
            table.at[BACK - step],
            kv_send.at[at, step - 1],
            kv_recv.at[at, step - 1],
            **holder(rows_at + step),
        )
        for step in range(1, BACK + 1)
        for at, table in enumerate((keys, values))
    ]
    go(kv_copies)
    project((1, 3), 2, 1)
    w_wait(4)
    project((4, 1), 0, 1)
    project((4, 1), 1, 2)
    project((4, 1), 2, 1)
    arrive(kv_copies)

    def attend(chunk, head):
        columns_here = pl.ds(pl.multiple_of(head * HEAD_DIM, HEAD_DIM), HEAD_DIM)
        tile = 256
        tiles = range(ROWS // tile)
        spans = [slice(r * tile, (r + 1) * tile) for r in tiles]
        query = [acc[chunk, spans[r], columns_here].astype(jnp.bfloat16) for r in tiles]
        run_max = [jnp.full((tile, 1), NEG_FLOOR, jnp.float32) for r in tiles]
        sums = [jnp.zeros((tile, 128), jnp.float32) for r in tiles]
        output = [jnp.zeros((tile, HEAD_DIM), jnp.float32) for r in tiles]
        for j in range(BACK + 1):
            for r in tiles:
                low = r * tile if j == 0 else 0
                high = (r + 1) * tile if j == BACK else STEP
                scores = jnp.dot(
                    query[r], keys[j, :, low:high], preferred_element_type=jnp.float32
                )
                scores = scores * SCALING + bias[j, spans[r], low:high]
                new_max = jnp.maximum(run_max[r], jnp.max(scores, axis=-1, keepdims=True))
                rescale = jnp.exp2(run_max[r] - new_max)
                probs = jnp.exp2(scores - new_max)
                output[r] = output[r] * rescale + jnp.dot(
                    probs.astype(jnp.bfloat16),
                    values[j, low:high, :],
                    preferred_element_type=jnp.float32,
                )
                partial = probs[:, :128]
                for first in range(128, high - low, 128):
                    partial = partial + probs[:, first : first + 128]
                sums[r] = sums[r] * rescale + partial
                run_max[r] = new_max
        for r in tiles:
            total = jnp.sum(sums[r], axis=-1, keepdims=True)
            attended[spans[r], columns_here] = (output[r] / total).astype(jnp.bfloat16)

    own_rows = pl.ds(pl.multiple_of(rows_at * BLOCK, BLOCK), BLOCK)

    def slot_copy(at, span, index, step):
        target = (rows_at + step) % LAYERS
        return remote(
            slots.at[at, pl.ds(pl.multiple_of(target * BLOCK, BLOCK), BLOCK), span],
            landed.at[at, own_rows, span],
            s_send.at[index, step],
            s_recv.at[index, step],
            layer=target,
            attn=group,
        )

    def slot_send(at, first, width, index):
        span = pl.ds(first, width)
        slots[at, :, span] = jnp.dot(
            pick[...], attended[:, span], preferred_element_type=jnp.float32
        ).astype(jnp.bfloat16)
        for step in range(1, LAYERS):
            slot_copy(at, span, index, step).start()
        own = slot_copy(at, span, index, 0)

        @pl.when(away)
        def _():
            own.start()

        @pl.when(home)
        def _():
            landed[at, own_rows, span] = slots[at, own_rows, span]

    def slot_take(at, first, width, index, column):
        span = pl.ds(first, width)
        for step in range(1, LAYERS):
            slot_copy(at, span, index, step).wait()
        own = slot_copy(at, span, index, 0)

        @pl.when(away)
        def _():
            own.wait()

        out_ref[:, pl.ds(column, width)] = jnp.dot(
            keep[...], landed[at, :, span], preferred_element_type=jnp.float32
        ).astype(jnp.bfloat16)

    @pl.loop(0, CHUNKS - 2)
    def _(at):
        @pl.loop(0, 2)
        def _(head):
            attend(at + 1, head)

        slot_send(at, 0, WIDE, at)

        @pl.when(at > 0)
        def _():
            slot_take(at - 1, 0, WIDE, at - 1, pl.multiple_of((at - 1) * WIDE, WIDE))

    last = CHUNKS - 2
    for head in range(2):
        attend(last + 1, head)
        slot_send(last, head * HEAD_DIM, HEAD_DIM, last + head)
        if head == 0:
            slot_take(last - 1, 0, WIDE, last - 1, (last - 1) * WIDE)
    for head in range(2):
        slot_take(
            last, head * HEAD_DIM, HEAD_DIM, last + head, last * WIDE + head * HEAD_DIM
        )

    for who, copies in sent.items():

        def done(copies=copies):
            for copy in copies:
                copy.wait_send()

        if who == "all":
            done()
        else:
            pl.when(condition[who])(done)


def fused(tokens, gain, weight, docs, plan):
    vmem = pl.BlockSpec(memory_space=pltpu.VMEM)
    dma = pltpu.SemaphoreType.DMA
    bf16, f32 = jnp.bfloat16, jnp.float32
    return pl.pallas_call(
        fused_kernel,
        out_shape=jax.ShapeDtypeStruct((ROWS, GROUP * HEAD_DIM), bf16),
        in_specs=[
            vmem,
            vmem,
            pl.BlockSpec(memory_space=pl.ANY),
            vmem,
            pl.BlockSpec(memory_space=pltpu.SMEM),
        ],
        out_specs=vmem,
        scratch_shapes=[
            pltpu.VMEM((ROWS, COLS), bf16),
            pltpu.VMEM((ATTN, ROWS, COLS), bf16),
            pltpu.VMEM((CHUNKS, 2, RING, 2, 2, HALF, WIDE), bf16),
            pltpu.VMEM((BACK + 1, HEAD_DIM, STEP), bf16),
            pltpu.VMEM((BACK + 1, STEP, HEAD_DIM), bf16),
            pltpu.VMEM((BACK + 1, ROWS, STEP), f32),
            pltpu.VMEM((LAYERS * BLOCK, ROWS), bf16),
            pltpu.VMEM((ROWS, LAYERS * BLOCK), bf16),
            pltpu.VMEM((ROWS, WIDE), bf16),
            pltpu.VMEM((CHUNKS - 1, LAYERS * BLOCK, WIDE), bf16),
            pltpu.VMEM((CHUNKS - 1, LAYERS * BLOCK, WIDE), bf16),
            pltpu.VMEM((CHUNKS, ROWS, WIDE), f32),
            pltpu.VMEM((ATTN, 8, ROWS), f32),
            dma((CHUNKS,)),
            dma((CHUNKS, 2)),
            dma((CHUNKS, 2)),
            dma((CHUNKS, 8)),
            dma((CHUNKS, 8)),
            dma((CHUNKS, 4)),
            dma((CHUNKS, 4)),
            dma((2, 2)),
            dma((2, 2)),
            dma((6,)),
            dma((6,)),
            dma((ATTN - 1,)),
            dma((ATTN - 1,)),
            dma((2, BACK)),
            dma((2, BACK)),
            dma((CHUNKS, LAYERS)),
            dma((CHUNKS, LAYERS)),
        ],
        compiler_params=pltpu.CompilerParams(
            collective_id=0, has_side_effects=True, vmem_limit_bytes=60 * 2**20
        ),
        cost_estimate=pl.CostEstimate(
            flops=2 * ROWS * 8192 * 1280, bytes_accessed=30 * 2**20, transcendentals=10 * 2**20
        ),
    )(tokens, gain, weight, docs, plan)


def solution(mesh):
    placed = (P("layer", "attn"), P(), P("layer", "attn"), P(), P())
    return jax.shard_map(
        fused, mesh=mesh, in_specs=placed, out_specs=P("layer", "attn"), check_vma=False
    )
```

```python
import math

import jax
import jax.numpy as jnp
from jax import lax
from jax.experimental import pallas as pl
from jax.experimental.pallas import tpu as pltpu
from jax.sharding import PartitionSpec as P

MESH = pl.DeviceIdType.MESH
HEAD_DIM = 128
GROUP = 8
BLOCK = 64
STEP = 512
BACK = 4
RING = 4
LAYERS = 16
ATTN = 8
ROWS = 512
COLS = 1024
WIDE = 256
CHUNKS = 5
HALF = 256

EPSILON = 1e-05
LOG2E = math.log2(math.e)
NEG_FLOOR = -1e30 * LOG2E
MASKED = -3e38
SCALING = LOG2E / math.sqrt(HEAD_DIM)


def remote(src, dst, send_sem, recv_sem, **device):
    return pltpu.make_async_remote_copy(
        src_ref=src,
        dst_ref=dst,
        send_sem=send_sem,
        recv_sem=recv_sem,
        device_id=device,
        device_id_type=MESH,
    )


def fused_kernel(
    tok_ref,
    gain_ref,
    w_ref,
    doc_ref,
    plan_ref,
    out_ref,
    mine,
    normed,
    weights,
    keys,
    values,
    bias,
    pick,
    keep,
    attended,
    slots,
    landed,
    acc,
    moments,
    own_sem,
    pair_send,
    pair_recv,
    w_send,
    w_recv,
    core_send,
    core_recv,
    share_send,
    share_recv,
    t_send,
    t_recv,
    m_send,
    m_recv,
    kv_send,
    kv_recv,
    s_send,
    s_recv,
):
    layer = lax.axis_index("layer")
    attn = lax.axis_index("attn")
    x, y = layer // RING, layer % RING
    z, core = attn // 2, attn % 2
    side = y // 2
    partner = x * RING + 3 - y
    inner = x * RING + y + 1 - 2 * (y % 2)
    unit = ((y + 1) // 2) % 2
    same = 1 - (core - side) * (core - side)
    home, away = core == side, core != side
    rows_at = same * layer + (1 - same) * partner
    sibling = attn + 1 - 2 * core
    group = 2 * z + side

    def holder(row):
        row = row % LAYERS
        across, along = row // RING, row % RING
        inside = 1 - (along // 2 - side) * (along // 2 - side)
        along = inside * along + (1 - inside) * (3 - along)
        core_there = inside * side + (1 - inside) * (1 - side)
        return {"layer": across * RING + along, "attn": 2 * z + core_there}

    def across_x(step):
        return {"layer": ((x + step) % RING) * RING + y}

    def along_z(step):
        return {"attn": (attn + 2 * step) % ATTN}

    shift = (1, -1)
    sent = {"all": [], "home": [], "away": [], 0: [], 1: []}
    condition = {"home": home, "away": away, 0: core == 0, 1: core == 1}

    def go(copies, who="all"):
        if who == "all":
            for copy in copies:
                copy.start()
        else:

            @pl.when(condition[who])
            def _():
                for copy in copies:
                    copy.start()

        sent[who].extend(copies)

    def arrive(copies, who="all"):
        if who == "all":
            for copy in copies:
                copy.wait_recv()
        else:

            @pl.when(condition[who])
            def _():
                for copy in copies:
                    copy.wait_recv()

    barrier = pltpu.get_barrier_semaphore()
    for step in range(1, LAYERS):
        for at in (attn, sibling):
            pl.semaphore_signal(
                barrier,
                inc=1,
                device_id={"layer": (layer + step) % LAYERS, "attn": at},
                device_id_type=MESH,
            )
    for step in range(1, ATTN):
        pl.semaphore_signal(
            barrier, inc=1, device_id={"attn": (attn + step) % ATTN}, device_id_type=MESH
        )
    pl.semaphore_wait(barrier, 2 * (LAYERS - 1) + ATTN - 1)

    def columns(chunk):
        first = GROUP * HEAD_DIM if chunk == 0 else (chunk - 1) * WIDE
        return pl.ds(first, WIDE)

    def w_pair(chunk):
        def share(half):
            rows = pl.ds(pl.multiple_of(half * HALF, HALF), HALF)
            return w_ref.at[rows, columns(chunk)], weights.at[chunk, half, x, unit, side]

        src, dst = share(1 - core)
        go(
            [
                remote(
                    src,
                    dst,
                    pair_send.at[chunk, 0],
                    pair_recv.at[chunk, 1 - same],
                    layer=rows_at,
                    attn=sibling,
                )
            ]
        )
        src, dst = share(core)
        go(
            [
                remote(
                    src,
                    dst,
                    pair_send.at[chunk, 1],
                    pair_recv.at[chunk, 1],
                    layer=partner,
                    attn=attn,
                )
            ],
            "away",
        )
        own = pltpu.make_async_copy(src, dst, own_sem.at[chunk])

        @pl.when(home)
        def _():
            own.start()

        return own

    def w_legs(chunk):
        ring = [across_x(shift[way]) for way in range(2)]
        cols = [x, (x - 1) % RING, (x + 1) % RING, (x + 2) % RING]

        def leg(ref, index, device):
            return remote(
                ref, ref, w_send.at[chunk, index], w_recv.at[chunk, index], **device
            )

        inside = {"layer": inner}
        first = {0: {}, 1: {}}
        units = [weights.at[chunk, 0, cols[k], unit] for k in range(4)]
        first[0]["near"] = [leg(units[0], way, ring[way]) for way in range(2)]
        first[0]["far"] = [
            leg(weights.at[chunk, 0, cols[1 + way], unit, way], 3 + way, ring[way])
            for way in range(2)
        ]
        first[0]["inner"] = [leg(units[k], (2, 5, 6, 7)[k], inside) for k in range(4)]
        first[1]["inner"] = [leg(weights.at[chunk, 1, x, unit], 0, inside)]
        first[1]["near"] = [leg(weights.at[chunk, 1, x], 1 + way, ring[way]) for way in range(2)]
        first[1]["far"] = [
            leg(weights.at[chunk, 1, cols[1 + way], way], 3 + way, ring[way]) for way in range(2)
        ]
        first["core"] = [
            remote(
                weights.at[chunk, core, cols[k]],
                weights.at[chunk, core, cols[k]],
                core_send.at[chunk, k],
                core_recv.at[chunk, k],
                attn=sibling,
            )
            for k in range(4)
        ]
        return first

    own_copies = {}
    legs = {}

    def w_start(chunk):
        own_copies[chunk] = w_pair(chunk)

    def w_one(chunk):
        legs[chunk] = w_legs(chunk)
        got = legs[chunk]
        place = weights.at[chunk, core, x, unit, side]
        from_core = remote(
            place, place, pair_send.at[chunk, 0], pair_recv.at[chunk, 0], attn=sibling
        )
        from_pair = remote(
            place, place, pair_send.at[chunk, 0], pair_recv.at[chunk, 1], layer=partner
        )

        @pl.when(home)
        def _():
            own_copies[chunk].wait()

        arrive([from_core], "away")
        arrive([from_pair])
        go([got[0]["near"][0], got[0]["near"][1], got[0]["inner"][0]], 0)
        go(got[1]["inner"], 1)

    def w_two(chunk):
        got = legs[chunk]
        for way in range(2):
            arrive([got[0]["near"][way]], 0)
            go([got[0]["far"][way], got[0]["inner"][1 + way]], 0)
        arrive(got[1]["inner"], 1)
        go(got[1]["near"] + [], 1)
        go([got["core"][0]], 1)

    def w_three(chunk):
        got = legs[chunk]
        arrive(got[0]["far"], 0)
        go([got[0]["inner"][3]], 0)
        for k in range(3):
            arrive([got[0]["inner"][k]], 0)
            go([got["core"][k]], 0)
        for way in range(2):
            arrive([got[1]["near"][way]], 1)
            go([got[1]["far"][way], got["core"][1 + way]], 1)

    def w_four(chunk):
        got = legs[chunk]
        arrive([got[0]["inner"][3]], 0)
        arrive(got[1]["far"], 1)
        go([got["core"][3]])

    def w_wait(chunk):
        arrive(legs[chunk]["core"])

    w_start(0)
    w_start(1)

    tokens = tok_ref[...].astype(jnp.float32)
    own_sum = jnp.sum(tokens * tokens, axis=1, keepdims=True)
    moments[attn] = jnp.transpose(jnp.broadcast_to(own_sum, (ROWS, 128)))[:8]
    m_copies = [
        remote(
            moments.at[attn],
            moments.at[attn],
            m_send.at[step - 1],
            m_recv.at[step - 1],
            attn=(attn + step) % ATTN,
        )
        for step in range(1, ATTN)
    ]
    go(m_copies)
    acc[...] = jnp.zeros_like(acc)
    arrive(m_copies)
    total = moments[0]
    for at in range(1, ATTN):
        total = total + moments[at]
    total = jnp.transpose(jnp.broadcast_to(total[:1], (128, ROWS)))[:, :1]
    scale = lax.rsqrt(total * (1.0 / (ATTN * COLS)) + EPSILON)
    gain = gain_ref[pl.ds(pl.multiple_of(attn * COLS, COLS), COLS)].reshape(1, COLS)
    mine[...] = (tok_ref[...].astype(jnp.float32) * scale * gain).astype(jnp.bfloat16)

    def share_copy(half, index, **device):
        rows = pl.ds(half * HALF, HALF)
        return remote(
            mine.at[rows],
            normed.at[attn, rows],
            share_send.at[index, half],
            share_recv.at[core, half],
            **device,
        )

    for half in range(2):
        go([share_copy(half, 0, layer=partner, attn=group)])
        go([share_copy(half, 1, attn=sibling)], "away")

    @pl.when(home)
    def _():
        normed[attn] = mine[...]

    def share_wait(which, half):
        rows = normed.at[2 * z + which, pl.ds(half * HALF, HALF)]
        return remote(
            rows, rows, share_send.at[0, half], share_recv.at[which, half], layer=partner
        )

    def z_rows(block, half):
        return normed.at[pl.ds(2 * (block % RING), 2), pl.ds(half * HALF, HALF)]

    def z_copy(ref, index, way):
        return remote(ref, ref, t_send.at[index], t_recv.at[index], **along_z(shift[way]))

    z_near = {
        (half, way): z_copy(z_rows(z, half), 2 * half + way, way)
        for half in range(2)
        for way in range(2)
    }
    z_far = [z_copy(z_rows(z - shift[way], way), 4 + way, way) for way in range(2)]
    share_pair = {half: [share_wait(0, half), share_wait(1, half)] for half in range(2)}
    share_core = {half: [share_wait(1 - core, half)] for half in range(2)}

    def z_start(who, half):
        arrive(share_core[half] if who == "home" else share_pair[half], who)
        go([z_near[half, 0], z_near[half, 1]], who)

    def z_forward(who, way):
        arrive([z_near[way, way]], who)
        go([z_far[way]], who)

    z_start("home", 0)
    z_start("home", 1)
    w_start(2)
    w_one(0)
    w_two(0)
    w_one(1)

    def one_hot(table, first, second, at):
        rows = table.shape[0]
        row_at = lax.broadcasted_iota(jnp.int32, (rows, 128), 0)
        col_at = lax.broadcasted_iota(jnp.int32, (rows, 128), 1)
        wanted = jnp.where(col_at < BLOCK, first, second)
        hit = (row_at // BLOCK == wanted) & (row_at % BLOCK == col_at % BLOCK)
        table[:, at * 128 : (at + 1) * 128] = jnp.where(hit, 1.0, 0.0).astype(jnp.bfloat16)

    blocks = ROWS // BLOCK
    for at in range(blocks // 2):
        first = rows_at * blocks + 2 * at
        one_hot(pick, plan_ref[first], plan_ref[first + 1], at)

    z_start("away", 0)
    w_three(0)
    w_two(1)

    places = []
    count = 0
    for source in range(LAYERS):
        present = 0
        for at in range(blocks):
            present = present + jnp.where(plan_ref[source * blocks + at] == layer, 1, 0)
        places.append(jnp.where(present == 1, count, -1))
        count = count + present
    for at in range(LAYERS // 2):
        one_hot(keep, places[2 * at], places[2 * at + 1], at)

    def doc_row(source):
        row = doc_ref[pl.ds(pl.multiple_of(source * STEP, STEP), STEP)]
        return row.reshape(1, STEP).astype(jnp.float32)

    row_doc = doc_row(rows_at)
    key_at = lax.broadcasted_iota(jnp.int32, (STEP, ROWS), 0)
    row_at = lax.broadcasted_iota(jnp.int32, (STEP, ROWS), 1)
    for j in range(BACK + 1):
        source = rows_at - BACK + j
        key_doc = doc_row((source + LAYERS) % LAYERS)
        key_doc = jnp.transpose(jnp.broadcast_to(key_doc, (128, STEP)))[:, :1]
        allowed = jnp.where(source < 0, -1.0, key_doc) == row_doc
        if j == BACK:
            allowed = allowed & (key_at <= row_at)
        bias[j] = jnp.where(allowed, 0.0, MASKED)

    def project(chunks, first, count):
        low, many = chunks
        stride = 2 if count == 2 else 1

        @pl.loop(0, 2 * count * many)
        def _(at):
            place = at % 2
            block = (z + first + stride * ((at // 2) % count)) % RING
            chunk = low + at // (2 * count)
            parts = [
                weights[chunk, half, block, spot, place]
                for spot in (place, 1 - place)
                for half in range(2)
            ]
            acc[chunk] += jnp.dot(
                normed[2 * block + place],
                jnp.concatenate(parts, axis=0),
                preferred_element_type=jnp.float32,
            )

    w_start(3)
    w_one(2)
    z_start("away", 1)
    w_four(0)
    z_forward("home", 0)
    z_forward("home", 1)
    w_three(1)
    w_two(2)
    w_start(4)
    w_one(3)
    w_wait(0)
    project((0, 1), 0, 1)
    w_four(1)
    w_three(2)
    w_two(3)
    w_one(4)
    w_wait(1)
    project((1, 1), 0, 1)
    z_forward("away", 0)
    z_forward("away", 1)
    w_four(2)
    w_three(3)
    w_two(4)
    for at in ((0, 1), (1, 0)):
        arrive([z_near[at]])
    project((0, 2), 1, 2)
    w_wait(2)
    project((2, 1), 0, 1)
    project((2, 1), 1, 2)
    w_four(3)
    w_three(4)
    arrive(z_far)

    project((0, 1), 2, 1)
    keys[BACK] = acc[0, :, :HEAD_DIM].astype(jnp.bfloat16)
    values[BACK] = jnp.transpose(acc[0, :, HEAD_DIM:]).astype(jnp.bfloat16)
    kv_copies = [
        remote(
            table.at[BACK],
            table.at[BACK - step],
            kv_send.at[at, step - 1],
            kv_recv.at[at, step - 1],
            **holder(rows_at + step),
        )
        for step in range(1, BACK + 1)
        for at, table in enumerate((keys, values))
    ]
    go(kv_copies)
    project((1, 2), 2, 1)
    w_wait(3)
    project((3, 1), 0, 4)
    arrive(kv_copies)

    def attend(chunk, head):
        columns_here = pl.ds(pl.multiple_of(head * HEAD_DIM, HEAD_DIM), HEAD_DIM)
        tile = 256
        tiles = range(ROWS // tile)
        spans = [slice(r * tile, (r + 1) * tile) for r in tiles]
        queries = jnp.transpose(acc[chunk, :, columns_here]).astype(jnp.bfloat16)
        run_max = [jnp.full((1, tile), NEG_FLOOR, jnp.float32) for r in tiles]
        sums = [jnp.zeros((1, tile), jnp.float32) for r in tiles]
        output = [jnp.zeros((HEAD_DIM, tile), jnp.float32) for r in tiles]
        for j in range(BACK + 1):
            for r in tiles:
                low = r * tile if j == 0 else 0
                high = (r + 1) * tile if j == BACK else STEP
                scores = jnp.dot(
                    keys[j, low:high, :], queries[:, spans[r]], preferred_element_type=jnp.float32
                )
                scores = scores * SCALING + bias[j, low:high, spans[r]]
                new_max = jnp.maximum(run_max[r], jnp.max(scores, axis=0, keepdims=True))
                rescale = jnp.exp2(run_max[r] - new_max)
                probs = jnp.exp2(scores - new_max)
                output[r] = output[r] * rescale + jnp.dot(
                    values[j, :, low:high],
                    probs.astype(jnp.bfloat16),
                    preferred_element_type=jnp.float32,
                )
                sums[r] = sums[r] * rescale + jnp.sum(probs, axis=0, keepdims=True)
                run_max[r] = new_max
        for r in tiles:
            attended[columns_here, spans[r]] = (output[r] / sums[r]).astype(jnp.bfloat16)

    own_rows = pl.ds(pl.multiple_of(rows_at * BLOCK, BLOCK), BLOCK)

    def slot_copy(at, span, index, step):
        target = (rows_at + step) % LAYERS
        return remote(
            slots.at[at, pl.ds(pl.multiple_of(target * BLOCK, BLOCK), BLOCK), span],
            landed.at[at, own_rows, span],
            s_send.at[index, step],
            s_recv.at[index, step],
            layer=target,
            attn=group,
        )

    def slot_send(at, first, width, index):
        span = pl.ds(first, width)
        slots[at, :, span] = lax.dot_general(
            pick[...],
            attended[span, :],
            (((1,), (1,)), ((), ())),
            preferred_element_type=jnp.float32,
        ).astype(jnp.bfloat16)
        for step in range(1, LAYERS):
            slot_copy(at, span, index, step).start()
        own = slot_copy(at, span, index, 0)

        @pl.when(away)
        def _():
            own.start()

        @pl.when(home)
        def _():
            landed[at, own_rows, span] = slots[at, own_rows, span]

    def slot_take(at, first, width, index, column):
        span = pl.ds(first, width)
        for step in range(1, LAYERS):
            slot_copy(at, span, index, step).wait()
        own = slot_copy(at, span, index, 0)

        @pl.when(away)
        def _():
            own.wait()

        out_ref[:, pl.ds(column, width)] = jnp.dot(
            keep[...], landed[at, :, span], preferred_element_type=jnp.float32
        ).astype(jnp.bfloat16)

    @pl.loop(0, CHUNKS - 2)
    def _(at):
        @pl.loop(0, 2)
        def _(head):
            attend(at + 1, head)

        slot_send(at, 0, WIDE, at)

        @pl.when(at == 0)
        def _():
            w_four(4)
            w_wait(4)
            project((4, 1), 0, 4)

        @pl.when(at > 0)
        def _():
            slot_take(at - 1, 0, WIDE, at - 1, pl.multiple_of((at - 1) * WIDE, WIDE))

    last = CHUNKS - 2
    for head in range(2):
        attend(last + 1, head)
        slot_send(last, head * HEAD_DIM, HEAD_DIM, last + head)
        if head == 0:
            slot_take(last - 1, 0, WIDE, last - 1, (last - 1) * WIDE)
    for head in range(2):
        slot_take(
            last, head * HEAD_DIM, HEAD_DIM, last + head, last * WIDE + head * HEAD_DIM
        )

    for who, copies in sent.items():

        def done(copies=copies):
            for copy in copies:
                copy.wait_send()

        if who == "all":
            done()
        else:
            pl.when(condition[who])(done)


def fused(tokens, gain, weight, docs, plan):
    vmem = pl.BlockSpec(memory_space=pltpu.VMEM)
    dma = pltpu.SemaphoreType.DMA
    bf16, f32 = jnp.bfloat16, jnp.float32
    return pl.pallas_call(
        fused_kernel,
        out_shape=jax.ShapeDtypeStruct((ROWS, GROUP * HEAD_DIM), bf16),
        in_specs=[
            vmem,
            vmem,
            pl.BlockSpec(memory_space=pl.ANY),
            vmem,
            pl.BlockSpec(memory_space=pltpu.SMEM),
        ],
        out_specs=vmem,
        scratch_shapes=[
            pltpu.VMEM((ROWS, COLS), bf16),
            pltpu.VMEM((ATTN, ROWS, COLS), bf16),
            pltpu.VMEM((CHUNKS, 2, RING, 2, 2, HALF, WIDE), bf16),
            pltpu.VMEM((BACK + 1, STEP, HEAD_DIM), bf16),
            pltpu.VMEM((BACK + 1, HEAD_DIM, STEP), bf16),
            pltpu.VMEM((BACK + 1, STEP, ROWS), f32),
            pltpu.VMEM((LAYERS * BLOCK, ROWS), bf16),
            pltpu.VMEM((ROWS, LAYERS * BLOCK), bf16),
            pltpu.VMEM((WIDE, ROWS), bf16),
            pltpu.VMEM((CHUNKS - 1, LAYERS * BLOCK, WIDE), bf16),
            pltpu.VMEM((CHUNKS - 1, LAYERS * BLOCK, WIDE), bf16),
            pltpu.VMEM((CHUNKS, ROWS, WIDE), f32),
            pltpu.VMEM((ATTN, 8, ROWS), f32),
            dma((CHUNKS,)),
            dma((CHUNKS, 2)),
            dma((CHUNKS, 2)),
            dma((CHUNKS, 8)),
            dma((CHUNKS, 8)),
            dma((CHUNKS, 4)),
            dma((CHUNKS, 4)),
            dma((2, 2)),
            dma((2, 2)),
            dma((6,)),
            dma((6,)),
            dma((ATTN - 1,)),
            dma((ATTN - 1,)),
            dma((2, BACK)),
            dma((2, BACK)),
            dma((CHUNKS, LAYERS)),
            dma((CHUNKS, LAYERS)),
        ],
        compiler_params=pltpu.CompilerParams(
            collective_id=0, has_side_effects=True, vmem_limit_bytes=60 * 2**20
        ),
        cost_estimate=pl.CostEstimate(
            flops=2 * ROWS * 8192 * 1280, bytes_accessed=30 * 2**20, transcendentals=10 * 2**20
        ),
    )(tokens, gain, weight, docs, plan)


def solution(mesh):
    placed = (P("layer", "attn"), P(), P("layer", "attn"), P(), P())
    return jax.shard_map(
        fused, mesh=mesh, in_specs=placed, out_specs=P("layer", "attn"), check_vma=False
    )
```

```python
import math

import jax
import jax.numpy as jnp
from jax import lax
from jax.experimental import pallas as pl
from jax.experimental.pallas import tpu as pltpu
from jax.sharding import PartitionSpec as P

MESH = pl.DeviceIdType.MESH
HEAD_DIM = 128
GROUP = 8
BLOCK = 64
STEP = 512
BACK = 4
RING = 4
LAYERS = 16
ATTN = 8
ROWS = 512
COLS = 1024
WIDE = 256
CHUNKS = 5
HALF = 256

EPSILON = 1e-05
LOG2E = math.log2(math.e)
NEG_FLOOR = -1e30 * LOG2E
MASKED = -3e38
SCALING = LOG2E / math.sqrt(HEAD_DIM)


def remote(src, dst, send_sem, recv_sem, **device):
    return pltpu.make_async_remote_copy(
        src_ref=src,
        dst_ref=dst,
        send_sem=send_sem,
        recv_sem=recv_sem,
        device_id=device,
        device_id_type=MESH,
    )


def fused_kernel(
    tok_ref,
    gain_ref,
    w_ref,
    doc_ref,
    plan_ref,
    out_ref,
    mine,
    normed,
    weights,
    keys,
    values,
    bias,
    pick,
    keep,
    attended,
    slots,
    landed,
    acc,
    moments,
    own_sem,
    pair_send,
    pair_recv,
    w_send,
    w_recv,
    core_send,
    core_recv,
    share_send,
    share_recv,
    t_send,
    t_recv,
    far_send,
    far_recv,
    m_send,
    m_recv,
    kv_send,
    kv_recv,
    s_send,
    s_recv,
):
    layer = lax.axis_index("layer")
    attn = lax.axis_index("attn")
    x, y = layer // RING, layer % RING
    z, core = attn // 2, attn % 2
    side = y // 2
    partner = x * RING + 3 - y
    inner = x * RING + y + 1 - 2 * (y % 2)
    unit = ((y + 1) // 2) % 2
    same = 1 - (core - side) * (core - side)
    home, away = core == side, core != side
    rows_at = same * layer + (1 - same) * partner
    sibling = attn + 1 - 2 * core
    group = 2 * z + side

    def holder(row):
        row = row % LAYERS
        across, along = row // RING, row % RING
        inside = 1 - (along // 2 - side) * (along // 2 - side)
        along = inside * along + (1 - inside) * (3 - along)
        core_there = inside * side + (1 - inside) * (1 - side)
        return {"layer": across * RING + along, "attn": 2 * z + core_there}

    def across_x(step):
        return {"layer": ((x + step) % RING) * RING + y}

    def along_z(step):
        return {"attn": (attn + 2 * step) % ATTN}

    shift = (1, -1)
    sent = {"all": [], "home": [], "away": [], 0: [], 1: []}
    condition = {"home": home, "away": away, 0: core == 0, 1: core == 1}

    def go(copies, who="all"):
        if who == "all":
            for copy in copies:
                copy.start()
        else:

            @pl.when(condition[who])
            def _():
                for copy in copies:
                    copy.start()

        sent[who].extend(copies)

    def arrive(copies, who="all"):
        if who == "all":
            for copy in copies:
                copy.wait_recv()
        else:

            @pl.when(condition[who])
            def _():
                for copy in copies:
                    copy.wait_recv()

    barrier = pltpu.get_barrier_semaphore()
    for step in range(1, LAYERS):
        for at in (attn, sibling):
            pl.semaphore_signal(
                barrier,
                inc=1,
                device_id={"layer": (layer + step) % LAYERS, "attn": at},
                device_id_type=MESH,
            )
    for step in range(1, ATTN):
        pl.semaphore_signal(
            barrier, inc=1, device_id={"attn": (attn + step) % ATTN}, device_id_type=MESH
        )
    pl.semaphore_wait(barrier, 2 * (LAYERS - 1) + ATTN - 1)

    def columns(chunk):
        first = GROUP * HEAD_DIM if chunk == 0 else (chunk - 1) * WIDE
        return pl.ds(first, WIDE)

    def w_pair(chunk):
        def share(half):
            rows = pl.ds(pl.multiple_of(half * HALF, HALF), HALF)
            return w_ref.at[rows, columns(chunk)], weights.at[chunk, half, x, unit, side]

        src, dst = share(1 - core)
        go(
            [
                remote(
                    src,
                    dst,
                    pair_send.at[chunk, 0],
                    pair_recv.at[chunk, 1 - same],
                    layer=rows_at,
                    attn=sibling,
                )
            ]
        )
        src, dst = share(core)
        go(
            [
                remote(
                    src,
                    dst,
                    pair_send.at[chunk, 1],
                    pair_recv.at[chunk, 1],
                    layer=partner,
                    attn=attn,
                )
            ],
            "away",
        )
        own = pltpu.make_async_copy(src, dst, own_sem.at[chunk])

        @pl.when(home)
        def _():
            own.start()

        return own

    def w_legs(chunk):
        ring = [across_x(shift[way]) for way in range(2)]
        cols = [x, (x - 1) % RING, (x + 1) % RING, (x + 2) % RING]

        def leg(ref, index, device):
            return remote(
                ref, ref, w_send.at[chunk, index], w_recv.at[chunk, index], **device
            )

        inside = {"layer": inner}
        first = {0: {}, 1: {}}
        units = [weights.at[chunk, 0, cols[k], unit] for k in range(4)]
        first[0]["near"] = [leg(units[0], way, ring[way]) for way in range(2)]
        first[0]["far"] = [
            leg(weights.at[chunk, 0, cols[1 + way], unit, way], 3 + way, ring[way])
            for way in range(2)
        ]
        first[0]["inner"] = [leg(units[k], (2, 5, 6, 7)[k], inside) for k in range(4)]
        first[1]["inner"] = [leg(weights.at[chunk, 1, x, unit], 0, inside)]
        first[1]["near"] = [leg(weights.at[chunk, 1, x], 1 + way, ring[way]) for way in range(2)]
        first[1]["far"] = [
            leg(weights.at[chunk, 1, cols[1 + way], way], 3 + way, ring[way]) for way in range(2)
        ]
        first["core"] = [
            remote(
                weights.at[chunk, core, cols[k]],
                weights.at[chunk, core, cols[k]],
                core_send.at[chunk, k],
                core_recv.at[chunk, k],
                attn=sibling,
            )
            for k in range(4)
        ]
        return first

    own_copies = {}
    legs = {}

    def w_start(chunk):
        own_copies[chunk] = w_pair(chunk)

    def w_one(chunk):
        legs[chunk] = w_legs(chunk)
        got = legs[chunk]
        place = weights.at[chunk, core, x, unit, side]
        from_core = remote(
            place, place, pair_send.at[chunk, 0], pair_recv.at[chunk, 0], attn=sibling
        )
        from_pair = remote(
            place, place, pair_send.at[chunk, 0], pair_recv.at[chunk, 1], layer=partner
        )

        @pl.when(home)
        def _():
            own_copies[chunk].wait()

        arrive([from_core], "away")
        arrive([from_pair])
        go([got[0]["near"][0], got[0]["near"][1], got[0]["inner"][0]], 0)
        go(got[1]["inner"], 1)

    def w_two(chunk):
        got = legs[chunk]
        for way in range(2):
            arrive([got[0]["near"][way]], 0)
            go([got[0]["far"][way], got[0]["inner"][1 + way]], 0)
        arrive(got[1]["inner"], 1)
        go(got[1]["near"] + [], 1)
        go([got["core"][0]], 1)

    def w_three(chunk):
        got = legs[chunk]
        arrive(got[0]["far"], 0)
        go([got[0]["inner"][3]], 0)
        for k in range(3):
            arrive([got[0]["inner"][k]], 0)
            go([got["core"][k]], 0)
        for way in range(2):
            arrive([got[1]["near"][way]], 1)
            go([got[1]["far"][way], got["core"][1 + way]], 1)

    def w_four(chunk):
        got = legs[chunk]
        arrive([got[0]["inner"][3]], 0)
        arrive(got[1]["far"], 1)
        go([got["core"][3]])

    def w_wait(chunk):
        arrive(legs[chunk]["core"])

    w_start(0)
    w_start(1)

    tokens = tok_ref[...].astype(jnp.float32)
    own_sum = jnp.sum(tokens * tokens, axis=1, keepdims=True)
    moments[attn] = jnp.transpose(jnp.broadcast_to(own_sum, (ROWS, 128)))[:8]
    m_copies = [
        remote(
            moments.at[attn],
            moments.at[attn],
            m_send.at[step - 1],
            m_recv.at[step - 1],
            attn=(attn + step) % ATTN,
        )
        for step in range(1, ATTN)
    ]
    go(m_copies)
    acc[...] = jnp.zeros_like(acc)
    arrive(m_copies)
    total = moments[0]
    for at in range(1, ATTN):
        total = total + moments[at]
    total = jnp.transpose(jnp.broadcast_to(total[:1], (128, ROWS)))[:, :1]
    scale = lax.rsqrt(total * (1.0 / (ATTN * COLS)) + EPSILON)
    gain = gain_ref[pl.ds(pl.multiple_of(attn * COLS, COLS), COLS)].reshape(1, COLS)
    mine[...] = (tok_ref[...].astype(jnp.float32) * scale * gain).astype(jnp.bfloat16)

    def share_copy(half, index, **device):
        rows = pl.ds(half * HALF, HALF)
        return remote(
            mine.at[rows],
            normed.at[attn, rows],
            share_send.at[index, half],
            share_recv.at[core, half],
            **device,
        )

    for half in range(2):
        go([share_copy(half, 0, layer=partner, attn=group)])
        go([share_copy(half, 1, attn=sibling)], "away")

    @pl.when(home)
    def _():
        normed[attn] = mine[...]

    def share_wait(which, half):
        rows = normed.at[2 * z + which, pl.ds(half * HALF, HALF)]
        return remote(
            rows, rows, share_send.at[0, half], share_recv.at[which, half], layer=partner
        )

    def z_rows(block, half):
        return normed.at[pl.ds(2 * (block % RING), 2), pl.ds(half * HALF, HALF)]

    def z_copy(ref, index, way):
        return remote(ref, ref, t_send.at[index], t_recv.at[index], **along_z(shift[way]))

    z_near = {
        (half, way): z_copy(z_rows(z, half), 2 * half + way, way)
        for half in range(2)
        for way in range(2)
    }
    z_far = [z_copy(z_rows(z - shift[way], way), 4 + way, way) for way in range(2)]
    pair_far = [
        remote(
            z_rows(z + 2, way),
            z_rows(z + 2, way),
            far_send.at[way],
            far_recv.at[way],
            layer=partner,
        )
        for way in range(2)
    ]
    share_pair = {half: [share_wait(0, half), share_wait(1, half)] for half in range(2)}
    share_core = {half: [share_wait(1 - core, half)] for half in range(2)}

    def z_start(who, half):
        arrive(share_core[half] if who == "home" else share_pair[half], who)
        go([z_near[half, 0], z_near[half, 1]], who)

    def z_forward(way):
        arrive([z_near[way, way]], "home")
        go([z_far[way]], "home")

    def z_partner(way):
        arrive([z_far[way]], "home")
        go([pair_far[way]], "home")

    z_start("home", 0)
    z_start("home", 1)
    w_one(0)
    w_two(0)
    w_start(2)
    w_one(1)

    def one_hot(table, first, second, at):
        rows = table.shape[0]
        row_at = lax.broadcasted_iota(jnp.int32, (rows, 128), 0)
        col_at = lax.broadcasted_iota(jnp.int32, (rows, 128), 1)
        wanted = jnp.where(col_at < BLOCK, first, second)
        hit = (row_at // BLOCK == wanted) & (row_at % BLOCK == col_at % BLOCK)
        table[:, at * 128 : (at + 1) * 128] = jnp.where(hit, 1.0, 0.0).astype(jnp.bfloat16)

    blocks = ROWS // BLOCK
    for at in range(blocks // 2):
        first = rows_at * blocks + 2 * at
        one_hot(pick, plan_ref[first], plan_ref[first + 1], at)

    places = []
    count = 0
    for source in range(LAYERS):
        present = 0
        for at in range(blocks):
            present = present + jnp.where(plan_ref[source * blocks + at] == layer, 1, 0)
        places.append(jnp.where(present == 1, count, -1))
        count = count + present
    for at in range(LAYERS // 2):
        one_hot(keep, places[2 * at], places[2 * at + 1], at)

    z_forward(0)
    w_three(0)
    w_two(1)
    z_start("away", 0)

    def doc_row(source):
        row = doc_ref[pl.ds(pl.multiple_of(source * STEP, STEP), STEP)]
        return row.reshape(1, STEP).astype(jnp.float32)

    row_doc = doc_row(rows_at)
    key_at = lax.broadcasted_iota(jnp.int32, (STEP, ROWS), 0)
    row_at = lax.broadcasted_iota(jnp.int32, (STEP, ROWS), 1)
    for j in range(BACK + 1):
        source = rows_at - BACK + j
        key_doc = doc_row((source + LAYERS) % LAYERS)
        key_doc = jnp.transpose(jnp.broadcast_to(key_doc, (128, STEP)))[:, :1]
        allowed = jnp.where(source < 0, -1.0, key_doc) == row_doc
        if j == BACK:
            allowed = allowed & (key_at <= row_at)
        bias[j] = jnp.where(allowed, 0.0, MASKED)

    def project(chunks, first, count):
        low, many = chunks
        stride = 2 if count == 2 else 1

        @pl.loop(0, 2 * count * many)
        def _(at):
            place = at % 2
            block = (z + first + stride * ((at // 2) % count)) % RING
            chunk = low + at // (2 * count)
            parts = [
                weights[chunk, half, block, spot, place]
                for spot in (place, 1 - place)
                for half in range(2)
            ]
            acc[chunk] += jnp.dot(
                normed[2 * block + place],
                jnp.concatenate(parts, axis=0),
                preferred_element_type=jnp.float32,
            )

    w_start(3)
    w_one(2)
    w_four(0)
    z_forward(1)
    z_start("away", 1)
    w_three(1)
    w_two(2)
    w_start(4)
    w_one(3)
    w_wait(0)
    project((0, 1), 0, 1)
    w_four(1)
    z_partner(0)
    w_three(2)
    w_two(3)
    w_one(4)
    w_wait(1)
    project((1, 1), 0, 1)
    z_partner(1)
    w_four(2)
    w_three(3)
    w_two(4)
    arrive([z_near[0, 0], z_near[1, 1]], "away")
    arrive([z_near[0, 1], z_near[1, 0]])
    project((0, 2), 1, 2)
    w_wait(2)
    project((2, 1), 0, 1)
    project((2, 1), 1, 2)
    w_four(3)
    arrive(pair_far, "away")

    project((0, 1), 2, 1)
    keys[BACK] = acc[0, :, :HEAD_DIM].astype(jnp.bfloat16)
    values[BACK] = jnp.transpose(acc[0, :, HEAD_DIM:]).astype(jnp.bfloat16)
    kv_copies = [
        remote(
            table.at[BACK],
            table.at[BACK - step],
            kv_send.at[at, step - 1],
            kv_recv.at[at, step - 1],
            **holder(rows_at + step),
        )
        for step in range(1, BACK + 1)
        for at, table in enumerate((keys, values))
    ]
    go(kv_copies)
    w_three(4)
    project((1, 2), 2, 1)
    w_wait(3)
    project((3, 1), 0, 4)
    arrive(kv_copies)

    def over_keys(combine, table):
        while table.shape[0] > 8:
            middle = table.shape[0] // 2
            table = combine(table[:middle], table[middle:])
        return table

    def attend(chunk, heads):
        tile = 256
        spans = [slice(r * tile, (r + 1) * tile) for r in range(ROWS // tile)]
        chains = [(head, r) for head in heads for r in range(ROWS // tile)]
        rows_of = {head: slice(head * HEAD_DIM, (head + 1) * HEAD_DIM) for head in heads}
        queries = {
            head: jnp.transpose(acc[chunk, :, rows_of[head]]).astype(jnp.bfloat16)
            for head in heads
        }
        run_max = {at: jnp.full((1, tile), NEG_FLOOR, jnp.float32) for at in chains}
        sums = {at: jnp.zeros((8, tile), jnp.float32) for at in chains}
        output = {at: jnp.zeros((HEAD_DIM, tile), jnp.float32) for at in chains}
        for j in range(BACK + 1):
            for at in chains:
                head, r = at
                low = r * tile if j == 0 else 0
                high = (r + 1) * tile if j == BACK else STEP
                scores = jnp.dot(
                    keys[j, low:high, :],
                    queries[head][:, spans[r]],
                    preferred_element_type=jnp.float32,
                )
                scores = scores * SCALING + bias[j, low:high, spans[r]]
                top = jnp.max(over_keys(jnp.maximum, scores), axis=0, keepdims=True)
                new_max = jnp.maximum(run_max[at], top)
                rescale = jnp.exp2(run_max[at] - new_max)
                probs = jnp.exp2(scores - new_max)
                output[at] = output[at] * rescale + jnp.dot(
                    values[j, :, low:high],
                    probs.astype(jnp.bfloat16),
                    preferred_element_type=jnp.float32,
                )
                sums[at] = sums[at] * rescale + over_keys(jnp.add, probs)
                run_max[at] = new_max
        for at in chains:
            head, r = at
            total = jnp.sum(sums[at], axis=0, keepdims=True)
            attended[rows_of[head], spans[r]] = (output[at] / total).astype(jnp.bfloat16)

    own_rows = pl.ds(pl.multiple_of(rows_at * BLOCK, BLOCK), BLOCK)

    def slot_copy(at, span, index, step):
        target = (rows_at + step) % LAYERS
        return remote(
            slots.at[at, pl.ds(pl.multiple_of(target * BLOCK, BLOCK), BLOCK), span],
            landed.at[at, own_rows, span],
            s_send.at[index, step],
            s_recv.at[index, step],
            layer=target,
            attn=group,
        )

    def slot_send(at, first, width, index):
        span = pl.ds(first, width)
        slots[at, :, span] = lax.dot_general(
            pick[...],
            attended[span, :],
            (((1,), (1,)), ((), ())),
            preferred_element_type=jnp.float32,
        ).astype(jnp.bfloat16)
        for step in range(1, LAYERS):
            slot_copy(at, span, index, step).start()
        own = slot_copy(at, span, index, 0)

        @pl.when(away)
        def _():
            own.start()

        @pl.when(home)
        def _():
            landed[at, own_rows, span] = slots[at, own_rows, span]

    def slot_take(at, first, width, index, column):
        span = pl.ds(first, width)
        for step in range(1, LAYERS):
            slot_copy(at, span, index, step).wait()
        own = slot_copy(at, span, index, 0)

        @pl.when(away)
        def _():
            own.wait()

        out_ref[:, pl.ds(column, width)] = jnp.dot(
            keep[...], landed[at, :, span], preferred_element_type=jnp.float32
        ).astype(jnp.bfloat16)

    @pl.loop(0, CHUNKS - 2)
    def _(at):
        attend(at + 1, (0, 1))
        slot_send(at, 0, WIDE, at)

        @pl.when(at == 0)
        def _():
            w_four(4)
            w_wait(4)
            project((4, 1), 0, 4)

        @pl.when(at > 0)
        def _():
            slot_take(at - 1, 0, WIDE, at - 1, pl.multiple_of((at - 1) * WIDE, WIDE))

    last = CHUNKS - 2
    for head in range(2):
        attend(last + 1, (head,))
        slot_send(last, head * HEAD_DIM, HEAD_DIM, last + head)
        if head == 0:
            slot_take(last - 1, 0, WIDE, last - 1, (last - 1) * WIDE)
    for head in range(2):
        slot_take(
            last, head * HEAD_DIM, HEAD_DIM, last + head, last * WIDE + head * HEAD_DIM
        )

    for who, copies in sent.items():

        def done(copies=copies):
            for copy in copies:
                copy.wait_send()

        if who == "all":
            done()
        else:
            pl.when(condition[who])(done)


def fused(tokens, gain, weight, docs, plan):
    vmem = pl.BlockSpec(memory_space=pltpu.VMEM)
    dma = pltpu.SemaphoreType.DMA
    bf16, f32 = jnp.bfloat16, jnp.float32
    return pl.pallas_call(
        fused_kernel,
        out_shape=jax.ShapeDtypeStruct((ROWS, GROUP * HEAD_DIM), bf16),
        in_specs=[
            vmem,
            vmem,
            pl.BlockSpec(memory_space=pl.ANY),
            vmem,
            pl.BlockSpec(memory_space=pltpu.SMEM),
        ],
        out_specs=vmem,
        scratch_shapes=[
            pltpu.VMEM((ROWS, COLS), bf16),
            pltpu.VMEM((ATTN, ROWS, COLS), bf16),
            pltpu.VMEM((CHUNKS, 2, RING, 2, 2, HALF, WIDE), bf16),
            pltpu.VMEM((BACK + 1, STEP, HEAD_DIM), bf16),
            pltpu.VMEM((BACK + 1, HEAD_DIM, STEP), bf16),
            pltpu.VMEM((BACK + 1, STEP, ROWS), f32),
            pltpu.VMEM((LAYERS * BLOCK, ROWS), bf16),
            pltpu.VMEM((ROWS, LAYERS * BLOCK), bf16),
            pltpu.VMEM((WIDE, ROWS), bf16),
            pltpu.VMEM((CHUNKS - 1, LAYERS * BLOCK, WIDE), bf16),
            pltpu.VMEM((CHUNKS - 1, LAYERS * BLOCK, WIDE), bf16),
            pltpu.VMEM((CHUNKS, ROWS, WIDE), f32),
            pltpu.VMEM((ATTN, 8, ROWS), f32),
            dma((CHUNKS,)),
            dma((CHUNKS, 2)),
            dma((CHUNKS, 2)),
            dma((CHUNKS, 8)),
            dma((CHUNKS, 8)),
            dma((CHUNKS, 4)),
            dma((CHUNKS, 4)),
            dma((2, 2)),
            dma((2, 2)),
            dma((6,)),
            dma((6,)),
            dma((2,)),
            dma((2,)),
            dma((ATTN - 1,)),
            dma((ATTN - 1,)),
            dma((2, BACK)),
            dma((2, BACK)),
            dma((CHUNKS, LAYERS)),
            dma((CHUNKS, LAYERS)),
        ],
        compiler_params=pltpu.CompilerParams(
            collective_id=0, has_side_effects=True, vmem_limit_bytes=60 * 2**20
        ),
        cost_estimate=pl.CostEstimate(
            flops=2 * ROWS * 8192 * 1280, bytes_accessed=30 * 2**20, transcendentals=10 * 2**20
        ),
    )(tokens, gain, weight, docs, plan)


def solution(mesh):
    placed = (P("layer", "attn"), P(), P("layer", "attn"), P(), P())
    return jax.shard_map(
        fused, mesh=mesh, in_specs=placed, out_specs=P("layer", "attn"), check_vma=False
    )
```

```python
import math

import jax
import jax.numpy as jnp
from jax import lax
from jax.experimental import pallas as pl
from jax.experimental.pallas import tpu as pltpu
from jax.sharding import PartitionSpec as P

MESH = pl.DeviceIdType.MESH
HEAD_DIM = 128
GROUP = 8
BLOCK = 64
STEP = 512
BACK = 4
RING = 4
LAYERS = 16
ATTN = 8
ROWS = 512
COLS = 1024
WIDE = 256
CHUNKS = 5
HALF = 256

EPSILON = 1e-05
LOG2E = math.log2(math.e)
NEG_FLOOR = -1e30 * LOG2E
MASKED = -3e38
SCALING = LOG2E / math.sqrt(HEAD_DIM)


def remote(src, dst, send_sem, recv_sem, **device):
    return pltpu.make_async_remote_copy(
        src_ref=src,
        dst_ref=dst,
        send_sem=send_sem,
        recv_sem=recv_sem,
        device_id=device,
        device_id_type=MESH,
    )


def fused_kernel(
    tok_ref,
    gain_ref,
    w_ref,
    doc_ref,
    plan_ref,
    out_ref,
    mine,
    normed,
    weights,
    keys,
    values,
    bias,
    pick,
    keep,
    attended,
    slots,
    landed,
    acc,
    moments,
    own_sem,
    pair_send,
    pair_recv,
    w_send,
    w_recv,
    core_send,
    core_recv,
    share_send,
    share_recv,
    t_send,
    t_recv,
    m_send,
    m_recv,
    kv_send,
    kv_recv,
    s_send,
    s_recv,
):
    layer = lax.axis_index("layer")
    attn = lax.axis_index("attn")
    x, y = layer // RING, layer % RING
    z, core = attn // 2, attn % 2
    side = y // 2
    partner = x * RING + 3 - y
    inner = x * RING + y + 1 - 2 * (y % 2)
    unit = ((y + 1) // 2) % 2
    same = 1 - (core - side) * (core - side)
    home, away = core == side, core != side
    rows_at = same * layer + (1 - same) * partner
    sibling = attn + 1 - 2 * core
    group = 2 * z + side

    def holder(row):
        row = row % LAYERS
        across, along = row // RING, row % RING
        inside = 1 - (along // 2 - side) * (along // 2 - side)
        along = inside * along + (1 - inside) * (3 - along)
        core_there = inside * side + (1 - inside) * (1 - side)
        return {"layer": across * RING + along, "attn": 2 * z + core_there}

    def across_x(step):
        return {"layer": ((x + step) % RING) * RING + y}

    def along_z(step):
        return {"attn": (attn + 2 * step) % ATTN}

    shift = (1, -1)
    sent = {"all": [], "home": [], "away": [], 0: [], 1: []}
    condition = {"home": home, "away": away, 0: core == 0, 1: core == 1}

    def go(copies, who="all"):
        if who == "all":
            for copy in copies:
                copy.start()
        else:

            @pl.when(condition[who])
            def _():
                for copy in copies:
                    copy.start()

        sent[who].extend(copies)

    def arrive(copies, who="all"):
        if who == "all":
            for copy in copies:
                copy.wait_recv()
        else:

            @pl.when(condition[who])
            def _():
                for copy in copies:
                    copy.wait_recv()

    barrier = pltpu.get_barrier_semaphore()
    for step in range(1, LAYERS):
        for at in (attn, sibling):
            pl.semaphore_signal(
                barrier,
                inc=1,
                device_id={"layer": (layer + step) % LAYERS, "attn": at},
                device_id_type=MESH,
            )
    for step in range(1, ATTN):
        pl.semaphore_signal(
            barrier, inc=1, device_id={"attn": (attn + step) % ATTN}, device_id_type=MESH
        )
    pl.semaphore_wait(barrier, 2 * (LAYERS - 1) + ATTN - 1)

    def columns(chunk):
        first = GROUP * HEAD_DIM if chunk == 0 else (chunk - 1) * WIDE
        return pl.ds(first, WIDE)

    def w_pair(chunk):
        def share(half):
            rows = pl.ds(pl.multiple_of(half * HALF, HALF), HALF)
            return w_ref.at[rows, columns(chunk)], weights.at[chunk, half, x, unit, side]

        src, dst = share(1 - core)
        go(
            [
                remote(
                    src,
                    dst,
                    pair_send.at[chunk, 0],
                    pair_recv.at[chunk, 1 - same],
                    layer=rows_at,
                    attn=sibling,
                )
            ]
        )
        src, dst = share(core)
        go(
            [
                remote(
                    src,
                    dst,
                    pair_send.at[chunk, 1],
                    pair_recv.at[chunk, 1],
                    layer=partner,
                    attn=attn,
                )
            ],
            "away",
        )
        own = pltpu.make_async_copy(src, dst, own_sem.at[chunk])

        @pl.when(home)
        def _():
            own.start()

        return own

    def w_legs(chunk):
        ring = [across_x(shift[way]) for way in range(2)]
        cols = [x, (x - 1) % RING, (x + 1) % RING, (x + 2) % RING]

        def leg(ref, index, device):
            return remote(
                ref, ref, w_send.at[chunk, index], w_recv.at[chunk, index], **device
            )

        inside = {"layer": inner}
        first = {0: {}, 1: {}}
        units = [weights.at[chunk, 0, cols[k], unit] for k in range(4)]
        first[0]["near"] = [leg(units[0], way, ring[way]) for way in range(2)]
        first[0]["far"] = [
            leg(weights.at[chunk, 0, cols[1 + way], unit, way], 3 + way, ring[way])
            for way in range(2)
        ]
        first[0]["inner"] = [leg(units[k], (2, 5, 6, 7)[k], inside) for k in range(4)]
        first[1]["inner"] = [leg(weights.at[chunk, 1, x, unit], 0, inside)]
        first[1]["near"] = [leg(weights.at[chunk, 1, x], 1 + way, ring[way]) for way in range(2)]
        first[1]["far"] = [
            leg(weights.at[chunk, 1, cols[1 + way], way], 3 + way, ring[way]) for way in range(2)
        ]
        first["core"] = [
            remote(
                weights.at[chunk, core, cols[k]],
                weights.at[chunk, core, cols[k]],
                core_send.at[chunk, k],
                core_recv.at[chunk, k],
                attn=sibling,
            )
            for k in range(4)
        ]
        return first

    own_copies = {}
    legs = {}

    def w_start(chunk):
        own_copies[chunk] = w_pair(chunk)

    def w_one(chunk):
        legs[chunk] = w_legs(chunk)
        got = legs[chunk]
        place = weights.at[chunk, core, x, unit, side]
        from_core = remote(
            place, place, pair_send.at[chunk, 0], pair_recv.at[chunk, 0], attn=sibling
        )
        from_pair = remote(
            place, place, pair_send.at[chunk, 0], pair_recv.at[chunk, 1], layer=partner
        )

        @pl.when(home)
        def _():
            own_copies[chunk].wait()

        arrive([from_core], "away")
        arrive([from_pair])
        go([got[0]["near"][0], got[0]["near"][1], got[0]["inner"][0]], 0)
        go(got[1]["inner"], 1)

    def w_two(chunk):
        got = legs[chunk]
        for way in range(2):
            arrive([got[0]["near"][way]], 0)
            go([got[0]["far"][way], got[0]["inner"][1 + way]], 0)
        arrive(got[1]["inner"], 1)
        go(got[1]["near"] + [], 1)
        go([got["core"][0]], 1)

    def w_three(chunk):
        got = legs[chunk]
        arrive(got[0]["far"], 0)
        go([got[0]["inner"][3]], 0)
        for k in range(3):
            arrive([got[0]["inner"][k]], 0)
            go([got["core"][k]], 0)
        for way in range(2):
            arrive([got[1]["near"][way]], 1)
            go([got[1]["far"][way], got["core"][1 + way]], 1)

    def w_four(chunk):
        got = legs[chunk]
        arrive([got[0]["inner"][3]], 0)
        arrive(got[1]["far"], 1)
        go([got["core"][3]])

    def w_wait(chunk):
        arrive(legs[chunk]["core"])

    w_start(0)
    w_start(1)
    w_start(2)

    tokens = tok_ref[...].astype(jnp.float32)
    own_sum = jnp.sum(tokens * tokens, axis=1, keepdims=True)
    moments[attn] = jnp.transpose(jnp.broadcast_to(own_sum, (ROWS, 128)))[:8]
    m_copies = [
        remote(
            moments.at[attn],
            moments.at[attn],
            m_send.at[step - 1],
            m_recv.at[step - 1],
            attn=(attn + step) % ATTN,
        )
        for step in range(1, ATTN)
    ]
    go(m_copies)
    acc[...] = jnp.zeros_like(acc)
    arrive(m_copies)
    total = moments[0]
    for at in range(1, ATTN):
        total = total + moments[at]
    total = jnp.transpose(jnp.broadcast_to(total[:1], (128, ROWS)))[:, :1]
    scale = lax.rsqrt(total * (1.0 / (ATTN * COLS)) + EPSILON)
    gain = gain_ref[pl.ds(pl.multiple_of(attn * COLS, COLS), COLS)].reshape(1, COLS)
    mine[...] = (tok_ref[...].astype(jnp.float32) * scale * gain).astype(jnp.bfloat16)

    def share_copy(half, index, **device):
        rows = pl.ds(half * HALF, HALF)
        return remote(
            mine.at[rows],
            normed.at[attn, rows],
            share_send.at[index, half],
            share_recv.at[core, half],
            **device,
        )

    for half in range(2):
        go([share_copy(half, 0, layer=partner, attn=group)])
        go([share_copy(half, 1, attn=sibling)], "away")

    @pl.when(home)
    def _():
        normed[attn] = mine[...]

    def share_wait(which, half):
        rows = normed.at[2 * z + which, pl.ds(half * HALF, HALF)]
        return remote(
            rows, rows, share_send.at[0, half], share_recv.at[which, half], layer=partner
        )

    def z_rows(block, half):
        return normed.at[pl.ds(2 * (block % RING), 2), pl.ds(half * HALF, HALF)]

    def z_copy(ref, index, way):
        return remote(ref, ref, t_send.at[index], t_recv.at[index], **along_z(shift[way]))

    z_near = {
        (half, way): z_copy(z_rows(z, half), 2 * half + way, way)
        for half in range(2)
        for way in range(2)
    }
    z_far = [z_copy(z_rows(z - shift[way], way), 4 + way, way) for way in range(2)]
    share_pair = {half: [share_wait(0, half), share_wait(1, half)] for half in range(2)}
    share_core = {half: [share_wait(1 - core, half)] for half in range(2)}

    def z_start(who, half):
        arrive(share_core[half] if who == "home" else share_pair[half], who)
        go([z_near[half, 0], z_near[half, 1]], who)

    def z_forward(who, way):
        arrive([z_near[way, way]], who)
        go([z_far[way]], who)

    z_start("home", 0)
    z_start("home", 1)
    w_one(0)
    w_two(0)
    w_one(1)

    def one_hot(table, first, second, at):
        rows = table.shape[0]
        row_at = lax.broadcasted_iota(jnp.int32, (rows, 128), 0)
        col_at = lax.broadcasted_iota(jnp.int32, (rows, 128), 1)
        wanted = jnp.where(col_at < BLOCK, first, second)
        hit = (row_at // BLOCK == wanted) & (row_at % BLOCK == col_at % BLOCK)
        table[:, at * 128 : (at + 1) * 128] = jnp.where(hit, 1.0, 0.0).astype(jnp.bfloat16)

    blocks = ROWS // BLOCK
    for at in range(blocks // 2):
        first = rows_at * blocks + 2 * at
        one_hot(pick, plan_ref[first], plan_ref[first + 1], at)

    z_start("away", 0)
    w_three(0)
    w_two(1)

    places = []
    count = 0
    for source in range(LAYERS):
        present = 0
        for at in range(blocks):
            present = present + jnp.where(plan_ref[source * blocks + at] == layer, 1, 0)
        places.append(jnp.where(present == 1, count, -1))
        count = count + present
    for at in range(LAYERS // 2):
        one_hot(keep, places[2 * at], places[2 * at + 1], at)

    def doc_row(source):
        row = doc_ref[pl.ds(pl.multiple_of(source * STEP, STEP), STEP)]
        return row.reshape(1, STEP).astype(jnp.float32)

    row_doc = jnp.transpose(jnp.broadcast_to(doc_row(rows_at), (128, STEP)))[:, :1]
    row_at = lax.broadcasted_iota(jnp.int32, (ROWS, STEP), 0)
    key_at = lax.broadcasted_iota(jnp.int32, (ROWS, STEP), 1)
    for j in range(BACK + 1):
        source = rows_at - BACK + j
        key_doc = doc_row((source + LAYERS) % LAYERS)
        allowed = jnp.where(source < 0, -1.0, key_doc) == row_doc
        if j == BACK:
            allowed = allowed & (key_at <= row_at)
        bias[j] = jnp.where(allowed, 0.0, MASKED)

    def project(chunks, first, count):
        low, many = chunks

        @pl.loop(0, 2 * count * many)
        def _(at):
            place = at % 2
            block = (z + first + 2 * ((at // 2) % count)) % RING
            chunk = low + at // (2 * count)
            parts = [
                weights[chunk, half, block, spot, place]
                for spot in (place, 1 - place)
                for half in range(2)
            ]
            acc[chunk] += jnp.dot(
                normed[2 * block + place],
                jnp.concatenate(parts, axis=0),
                preferred_element_type=jnp.float32,
            )

    w_start(3)
    w_one(2)
    z_start("away", 1)
    w_four(0)
    z_forward("home", 0)
    z_forward("home", 1)
    w_three(1)
    w_two(2)
    w_start(4)
    w_one(3)
    w_wait(0)
    project((0, 1), 0, 1)
    w_four(1)
    w_three(2)
    w_two(3)
    w_one(4)
    w_wait(1)
    project((1, 1), 0, 1)
    z_forward("away", 0)
    z_forward("away", 1)
    w_four(2)
    w_three(3)
    w_two(4)
    for at in ((0, 1), (1, 0)):
        arrive([z_near[at]])
    project((0, 2), 1, 2)
    w_four(3)
    w_three(4)
    w_wait(2)
    project((2, 1), 0, 1)
    project((2, 1), 1, 2)
    w_wait(3)
    project((3, 1), 0, 1)
    project((3, 1), 1, 2)
    w_four(4)
    arrive(z_far)

    project((0, 1), 2, 1)
    keys[BACK] = jnp.transpose(acc[0, :, :HEAD_DIM]).astype(jnp.bfloat16)
    values[BACK] = acc[0, :, HEAD_DIM:].astype(jnp.bfloat16)
    kv_copies = [
        remote(
            table.at[BACK],
            table.at[BACK - step],
            kv_send.at[at, step - 1],
            kv_recv.at[at, step - 1],
            **holder(rows_at + step),
        )
        for step in range(1, BACK + 1)
        for at, table in enumerate((keys, values))
    ]
    go(kv_copies)
    project((1, 3), 2, 1)
    w_wait(4)
    project((4, 1), 0, 1)
    project((4, 1), 1, 2)
    project((4, 1), 2, 1)
    arrive(kv_copies)

    def attend(chunk, head):
        columns_here = pl.ds(pl.multiple_of(head * HEAD_DIM, HEAD_DIM), HEAD_DIM)
        tile = 256
        tiles = range(ROWS // tile)
        spans = [slice(r * tile, (r + 1) * tile) for r in tiles]
        query = [acc[chunk, spans[r], columns_here].astype(jnp.bfloat16) for r in tiles]
        run_max = [jnp.full((tile, 1), NEG_FLOOR, jnp.float32) for r in tiles]
        sums = [jnp.zeros((tile, 128), jnp.float32) for r in tiles]
        output = [jnp.zeros((tile, HEAD_DIM), jnp.float32) for r in tiles]
        for j in range(BACK + 1):
            for r in tiles:
                low = r * tile if j == 0 else 0
                high = (r + 1) * tile if j == BACK else STEP
                scores = jnp.dot(
                    query[r], keys[j, :, low:high], preferred_element_type=jnp.float32
                )
                scores = scores * SCALING + bias[j, spans[r], low:high]
                new_max = jnp.maximum(run_max[r], jnp.max(scores, axis=-1, keepdims=True))
                rescale = jnp.exp2(run_max[r] - new_max)
                probs = jnp.exp2(scores - new_max)
                output[r] = output[r] * rescale + jnp.dot(
                    probs.astype(jnp.bfloat16),
                    values[j, low:high, :],
                    preferred_element_type=jnp.float32,
                )
                partial = probs[:, :128]
                for first in range(128, high - low, 128):
                    partial = partial + probs[:, first : first + 128]
                sums[r] = sums[r] * rescale + partial
                run_max[r] = new_max
        for r in tiles:
            total = jnp.sum(sums[r], axis=-1, keepdims=True)
            attended[spans[r], columns_here] = (output[r] / total).astype(jnp.bfloat16)

    own_rows = pl.ds(pl.multiple_of(rows_at * BLOCK, BLOCK), BLOCK)

    def slot_copy(at, span, index, step):
        target = (rows_at + step) % LAYERS
        return remote(
            slots.at[at, pl.ds(pl.multiple_of(target * BLOCK, BLOCK), BLOCK), span],
            landed.at[at, own_rows, span],
            s_send.at[index, step],
            s_recv.at[index, step],
            layer=target,
            attn=group,
        )

    def slot_send(at, first, width, index):
        span = pl.ds(first, width)
        slots[at, :, span] = jnp.dot(
            pick[...], attended[:, span], preferred_element_type=jnp.float32
        ).astype(jnp.bfloat16)
        for step in range(1, LAYERS):
            slot_copy(at, span, index, step).start()
        own = slot_copy(at, span, index, 0)

        @pl.when(away)
        def _():
            own.start()

        @pl.when(home)
        def _():
            landed[at, own_rows, span] = slots[at, own_rows, span]

    def slot_take(at, first, width, index, column):
        span = pl.ds(first, width)
        for step in range(1, LAYERS):
            slot_copy(at, span, index, step).wait()
        own = slot_copy(at, span, index, 0)

        @pl.when(away)
        def _():
            own.wait()

        out_ref[:, pl.ds(column, width)] = jnp.dot(
            keep[...], landed[at, :, span], preferred_element_type=jnp.float32
        ).astype(jnp.bfloat16)

    @pl.loop(0, CHUNKS - 2)
    def _(at):
        @pl.loop(0, 2)
        def _(head):
            attend(at + 1, head)

        slot_send(at, 0, WIDE, at)

        @pl.when(at > 0)
        def _():
            slot_take(at - 1, 0, WIDE, at - 1, pl.multiple_of((at - 1) * WIDE, WIDE))

    last = CHUNKS - 2
    for head in range(2):
        attend(last + 1, head)
        slot_send(last, head * HEAD_DIM, HEAD_DIM, last + head)
        if head == 0:
            slot_take(last - 1, 0, WIDE, last - 1, (last - 1) * WIDE)
    for head in range(2):
        slot_take(
            last, head * HEAD_DIM, HEAD_DIM, last + head, last * WIDE + head * HEAD_DIM
        )

    for who, copies in sent.items():

        def done(copies=copies):
            for copy in copies:
                copy.wait_send()

        if who == "all":
            done()
        else:
            pl.when(condition[who])(done)


def fused(tokens, gain, weight, docs, plan):
    vmem = pl.BlockSpec(memory_space=pltpu.VMEM)
    dma = pltpu.SemaphoreType.DMA
    bf16, f32 = jnp.bfloat16, jnp.float32
    return pl.pallas_call(
        fused_kernel,
        out_shape=jax.ShapeDtypeStruct((ROWS, GROUP * HEAD_DIM), bf16),
        in_specs=[
            vmem,
            vmem,
            pl.BlockSpec(memory_space=pl.ANY),
            vmem,
            pl.BlockSpec(memory_space=pltpu.SMEM),
        ],
        out_specs=vmem,
        scratch_shapes=[
            pltpu.VMEM((ROWS, COLS), bf16),
            pltpu.VMEM((ATTN, ROWS, COLS), bf16),
            pltpu.VMEM((CHUNKS, 2, RING, 2, 2, HALF, WIDE), bf16),
            pltpu.VMEM((BACK + 1, HEAD_DIM, STEP), bf16),
            pltpu.VMEM((BACK + 1, STEP, HEAD_DIM), bf16),
            pltpu.VMEM((BACK + 1, ROWS, STEP), f32),
            pltpu.VMEM((LAYERS * BLOCK, ROWS), bf16),
            pltpu.VMEM((ROWS, LAYERS * BLOCK), bf16),
            pltpu.VMEM((ROWS, WIDE), bf16),
            pltpu.VMEM((CHUNKS - 1, LAYERS * BLOCK, WIDE), bf16),
            pltpu.VMEM((CHUNKS - 1, LAYERS * BLOCK, WIDE), bf16),
            pltpu.VMEM((CHUNKS, ROWS, WIDE), f32),
            pltpu.VMEM((ATTN, 8, ROWS), f32),
            dma((CHUNKS,)),
            dma((CHUNKS, 2)),
            dma((CHUNKS, 2)),
            dma((CHUNKS, 8)),
            dma((CHUNKS, 8)),
            dma((CHUNKS, 4)),
            dma((CHUNKS, 4)),
            dma((2, 2)),
            dma((2, 2)),
            dma((6,)),
            dma((6,)),
            dma((ATTN - 1,)),
            dma((ATTN - 1,)),
            dma((2, BACK)),
            dma((2, BACK)),
            dma((CHUNKS, LAYERS)),
            dma((CHUNKS, LAYERS)),
        ],
        compiler_params=pltpu.CompilerParams(
            collective_id=0, has_side_effects=True, vmem_limit_bytes=60 * 2**20
        ),
        cost_estimate=pl.CostEstimate(
            flops=2 * ROWS * 8192 * 1280, bytes_accessed=30 * 2**20, transcendentals=10 * 2**20
        ),
    )(tokens, gain, weight, docs, plan)


def solution(mesh):
    placed = (P("layer", "attn"), P(), P("layer", "attn"), P(), P())
    return jax.shard_map(
        fused, mesh=mesh, in_specs=placed, out_specs=P("layer", "attn"), check_vma=False
    )
```

```python
import math

import jax
import jax.numpy as jnp
from jax import lax
from jax.experimental import pallas as pl
from jax.experimental.pallas import tpu as pltpu
from jax.sharding import PartitionSpec as P

MESH = pl.DeviceIdType.MESH
HEAD_DIM = 128
GROUP = 8
BLOCK = 64
STEP = 512
BACK = 4
RING = 4
LAYERS = 16
ATTN = 8
ROWS = 512
COLS = 1024
WIDE = 256
CHUNKS = 5
HALF = 256

EPSILON = 1e-05
LOG2E = math.log2(math.e)
NEG_FLOOR = -1e30 * LOG2E
MASKED = -3e38
SCALING = LOG2E / math.sqrt(HEAD_DIM)


def remote(src, dst, send_sem, recv_sem, **device):
    return pltpu.make_async_remote_copy(
        src_ref=src,
        dst_ref=dst,
        send_sem=send_sem,
        recv_sem=recv_sem,
        device_id=device,
        device_id_type=MESH,
    )


def fused_kernel(
    tok_ref,
    gain_ref,
    w_ref,
    doc_ref,
    plan_ref,
    out_ref,
    mine,
    normed,
    weights,
    keys,
    values,
    bias,
    pick,
    keep,
    attended,
    slots,
    landed,
    acc,
    moments,
    own_sem,
    pair_send,
    pair_recv,
    w_send,
    w_recv,
    core_send,
    core_recv,
    share_send,
    share_recv,
    t_send,
    t_recv,
    m_send,
    m_recv,
    kv_send,
    kv_recv,
    s_send,
    s_recv,
):
    layer = lax.axis_index("layer")
    attn = lax.axis_index("attn")
    x, y = layer // RING, layer % RING
    z, core = attn // 2, attn % 2
    side = y // 2
    partner = x * RING + 3 - y
    inner = x * RING + y + 1 - 2 * (y % 2)
    unit = ((y + 1) // 2) % 2
    same = 1 - (core - side) * (core - side)
    home, away = core == side, core != side
    rows_at = same * layer + (1 - same) * partner
    sibling = attn + 1 - 2 * core
    group = 2 * z + side

    def holder(row):
        row = row % LAYERS
        across, along = row // RING, row % RING
        inside = 1 - (along // 2 - side) * (along // 2 - side)
        along = inside * along + (1 - inside) * (3 - along)
        core_there = inside * side + (1 - inside) * (1 - side)
        return {"layer": across * RING + along, "attn": 2 * z + core_there}

    def across_x(step):
        return {"layer": ((x + step) % RING) * RING + y}

    def along_z(step):
        return {"attn": (attn + 2 * step) % ATTN}

    shift = (1, -1)
    sent = {"all": [], "home": [], "away": [], 0: [], 1: []}
    condition = {"home": home, "away": away, 0: core == 0, 1: core == 1}

    def go(copies, who="all"):
        if who == "all":
            for copy in copies:
                copy.start()
        else:

            @pl.when(condition[who])
            def _():
                for copy in copies:
                    copy.start()

        sent[who].extend(copies)

    def arrive(copies, who="all"):
        if who == "all":
            for copy in copies:
                copy.wait_recv()
        else:

            @pl.when(condition[who])
            def _():
                for copy in copies:
                    copy.wait_recv()

    barrier = pltpu.get_barrier_semaphore()
    for step in range(1, LAYERS):
        for at in (attn, sibling):
            pl.semaphore_signal(
                barrier,
                inc=1,
                device_id={"layer": (layer + step) % LAYERS, "attn": at},
                device_id_type=MESH,
            )
    for step in range(1, ATTN):
        pl.semaphore_signal(
            barrier, inc=1, device_id={"attn": (attn + step) % ATTN}, device_id_type=MESH
        )
    pl.semaphore_wait(barrier, 2 * (LAYERS - 1) + ATTN - 1)

    def columns(chunk):
        first = GROUP * HEAD_DIM if chunk == 0 else (chunk - 1) * WIDE
        return pl.ds(first, WIDE)

    def w_pair(chunk):
        def share(half):
            rows = pl.ds(pl.multiple_of(half * HALF, HALF), HALF)
            return w_ref.at[rows, columns(chunk)], weights.at[chunk, half, x, unit, side]

        src, dst = share(1 - core)
        go(
            [
                remote(
                    src,
                    dst,
                    pair_send.at[chunk, 0],
                    pair_recv.at[chunk, 1 - same],
                    layer=rows_at,
                    attn=sibling,
                )
            ]
        )
        src, dst = share(core)
        go(
            [
                remote(
                    src,
                    dst,
                    pair_send.at[chunk, 1],
                    pair_recv.at[chunk, 1],
                    layer=partner,
                    attn=attn,
                )
            ],
            "away",
        )
        own = pltpu.make_async_copy(src, dst, own_sem.at[chunk])

        @pl.when(home)
        def _():
            own.start()

        return own

    def w_legs(chunk):
        ring = [across_x(shift[way]) for way in range(2)]
        cols = [x, (x - 1) % RING, (x + 1) % RING, (x + 2) % RING]

        def leg(ref, index, device):
            return remote(
                ref, ref, w_send.at[chunk, index], w_recv.at[chunk, index], **device
            )

        inside = {"layer": inner}
        first = {0: {}, 1: {}}
        units = [weights.at[chunk, 0, cols[k], unit] for k in range(4)]
        first[0]["near"] = [leg(units[0], way, ring[way]) for way in range(2)]
        first[0]["far"] = [
            leg(weights.at[chunk, 0, cols[1 + way], unit, way], 3 + way, ring[way])
            for way in range(2)
        ]
        first[0]["inner"] = [leg(units[k], (2, 5, 6, 7)[k], inside) for k in range(4)]
        first[1]["inner"] = [leg(weights.at[chunk, 1, x, unit], 0, inside)]
        first[1]["near"] = [leg(weights.at[chunk, 1, x], 1 + way, ring[way]) for way in range(2)]
        first[1]["far"] = [
            leg(weights.at[chunk, 1, cols[1 + way], way], 3 + way, ring[way]) for way in range(2)
        ]
        first["core"] = [
            remote(
                weights.at[chunk, core, cols[k]],
                weights.at[chunk, core, cols[k]],
                core_send.at[chunk, k],
                core_recv.at[chunk, k],
                attn=sibling,
            )
            for k in range(4)
        ]
        return first

    own_copies = {}
    legs = {}

    def w_start(chunk):
        own_copies[chunk] = w_pair(chunk)

    def w_one(chunk):
        legs[chunk] = w_legs(chunk)
        got = legs[chunk]
        place = weights.at[chunk, core, x, unit, side]
        from_core = remote(
            place, place, pair_send.at[chunk, 0], pair_recv.at[chunk, 0], attn=sibling
        )
        from_pair = remote(
            place, place, pair_send.at[chunk, 0], pair_recv.at[chunk, 1], layer=partner
        )

        @pl.when(home)
        def _():
            own_copies[chunk].wait()

        arrive([from_core], "away")
        arrive([from_pair])
        go([got[0]["near"][0], got[0]["near"][1], got[0]["inner"][0]], 0)
        go(got[1]["inner"], 1)

    def w_two(chunk):
        got = legs[chunk]
        for way in range(2):
            arrive([got[0]["near"][way]], 0)
            go([got[0]["far"][way], got[0]["inner"][1 + way]], 0)
        arrive(got[1]["inner"], 1)
        go(got[1]["near"] + [], 1)
        go([got["core"][0]], 1)

    def w_three(chunk):
        got = legs[chunk]
        arrive(got[0]["far"], 0)
        go([got[0]["inner"][3]], 0)
        for k in range(3):
            arrive([got[0]["inner"][k]], 0)
            go([got["core"][k]], 0)
        for way in range(2):
            arrive([got[1]["near"][way]], 1)
            go([got[1]["far"][way], got["core"][1 + way]], 1)

    def w_four(chunk):
        got = legs[chunk]
        arrive([got[0]["inner"][3]], 0)
        arrive(got[1]["far"], 1)
        go([got["core"][3]])

    def w_wait(chunk):
        arrive(legs[chunk]["core"])

    w_start(0)
    w_start(1)
    w_start(2)

    tokens = tok_ref[...].astype(jnp.float32)
    own_sum = jnp.sum(tokens * tokens, axis=1, keepdims=True)
    moments[attn] = jnp.transpose(jnp.broadcast_to(own_sum, (ROWS, 128)))[:8]
    m_copies = [
        remote(
            moments.at[attn],
            moments.at[attn],
            m_send.at[step - 1],
            m_recv.at[step - 1],
            attn=(attn + step) % ATTN,
        )
        for step in range(1, ATTN)
    ]
    go(m_copies)
    acc[...] = jnp.zeros_like(acc)
    w_one(0)
    arrive(m_copies)
    total = moments[0]
    for at in range(1, ATTN):
        total = total + moments[at]
    total = jnp.transpose(jnp.broadcast_to(total[:1], (128, ROWS)))[:, :1]
    scale = lax.rsqrt(total * (1.0 / (ATTN * COLS)) + EPSILON)
    gain = gain_ref[pl.ds(pl.multiple_of(attn * COLS, COLS), COLS)].reshape(1, COLS)
    mine[...] = (tok_ref[...].astype(jnp.float32) * scale * gain).astype(jnp.bfloat16)

    def share_copy(half, index, **device):
        rows = pl.ds(half * HALF, HALF)
        return remote(
            mine.at[rows],
            normed.at[attn, rows],
            share_send.at[index, half],
            share_recv.at[core, half],
            **device,
        )

    for half in range(2):
        go([share_copy(half, 0, layer=partner, attn=group)])
        go([share_copy(half, 1, attn=sibling)], "away")

    @pl.when(home)
    def _():
        normed[attn] = mine[...]

    def share_wait(which, half):
        rows = normed.at[2 * z + which, pl.ds(half * HALF, HALF)]
        return remote(
            rows, rows, share_send.at[0, half], share_recv.at[which, half], layer=partner
        )

    def z_rows(block, half):
        return normed.at[pl.ds(2 * (block % RING), 2), pl.ds(half * HALF, HALF)]

    def z_copy(ref, index, way):
        return remote(ref, ref, t_send.at[index], t_recv.at[index], **along_z(shift[way]))

    z_near = {
        (half, way): z_copy(z_rows(z, half), 2 * half + way, way)
        for half in range(2)
        for way in range(2)
    }
    z_far = [z_copy(z_rows(z - shift[way], way), 4 + way, way) for way in range(2)]
    share_pair = {half: [share_wait(0, half), share_wait(1, half)] for half in range(2)}
    share_core = {half: [share_wait(1 - core, half)] for half in range(2)}

    def z_start(who, half):
        arrive(share_core[half] if who == "home" else share_pair[half], who)
        go([z_near[half, 0], z_near[half, 1]], who)

    def z_forward(who, way):
        arrive([z_near[way, way]], who)
        go([z_far[way]], who)

    z_start("home", 0)
    z_start("home", 1)
    w_two(0)
    w_one(1)

    def one_hot(table, first, second, at):
        rows = table.shape[0]
        row_at = lax.broadcasted_iota(jnp.int32, (rows, 128), 0)
        col_at = lax.broadcasted_iota(jnp.int32, (rows, 128), 1)
        wanted = jnp.where(col_at < BLOCK, first, second)
        hit = (row_at // BLOCK == wanted) & (row_at % BLOCK == col_at % BLOCK)
        table[:, at * 128 : (at + 1) * 128] = jnp.where(hit, 1.0, 0.0).astype(jnp.bfloat16)

    blocks = ROWS // BLOCK
    for at in range(blocks // 2):
        first = rows_at * blocks + 2 * at
        one_hot(pick, plan_ref[first], plan_ref[first + 1], at)

    z_start("away", 0)
    w_three(0)
    w_two(1)

    places = []
    count = 0
    for source in range(LAYERS):
        present = 0
        for at in range(blocks):
            present = present + jnp.where(plan_ref[source * blocks + at] == layer, 1, 0)
        places.append(jnp.where(present == 1, count, -1))
        count = count + present
    for at in range(LAYERS // 2):
        one_hot(keep, places[2 * at], places[2 * at + 1], at)

    def doc_row(source):
        row = doc_ref[pl.ds(pl.multiple_of(source * STEP, STEP), STEP)]
        return row.reshape(1, STEP).astype(jnp.float32)

    row_doc = jnp.transpose(jnp.broadcast_to(doc_row(rows_at), (128, STEP)))[:, :1]
    row_at = lax.broadcasted_iota(jnp.int32, (ROWS, STEP), 0)
    key_at = lax.broadcasted_iota(jnp.int32, (ROWS, STEP), 1)
    for j in range(BACK + 1):
        source = rows_at - BACK + j
        key_doc = doc_row((source + LAYERS) % LAYERS)
        allowed = jnp.where(source < 0, -1.0, key_doc) == row_doc
        if j == BACK:
            allowed = allowed & (key_at <= row_at)
        bias[j] = jnp.where(allowed, 0.0, MASKED)

    def project(chunks, first, count):
        low, many = chunks

        @pl.loop(0, 2 * count * many)
        def _(at):
            place = at % 2
            block = (z + first + 2 * ((at // 2) % count)) % RING
            chunk = low + at // (2 * count)
            parts = [
                weights[chunk, half, block, spot, place]
                for spot in (place, 1 - place)
                for half in range(2)
            ]
            acc[chunk] += jnp.dot(
                normed[2 * block + place],
                jnp.concatenate(parts, axis=0),
                preferred_element_type=jnp.float32,
            )

    w_start(3)
    w_one(2)
    z_start("away", 1)
    w_four(0)
    z_forward("home", 0)
    z_forward("home", 1)
    w_three(1)
    w_two(2)
    w_start(4)
    w_one(3)
    w_wait(0)
    project((0, 1), 0, 1)
    w_four(1)
    w_three(2)
    w_two(3)
    w_one(4)
    w_wait(1)
    project((1, 1), 0, 1)
    z_forward("away", 0)
    z_forward("away", 1)
    w_four(2)
    w_three(3)
    w_two(4)
    for at in ((0, 1), (1, 0)):
        arrive([z_near[at]])
    project((0, 2), 1, 2)
    w_four(3)
    w_three(4)
    w_wait(2)
    project((2, 1), 0, 1)
    project((2, 1), 1, 2)
    w_wait(3)
    project((3, 1), 0, 1)
    project((3, 1), 1, 2)
    w_four(4)
    arrive(z_far)

    project((0, 1), 2, 1)
    keys[BACK] = jnp.transpose(acc[0, :, :HEAD_DIM]).astype(jnp.bfloat16)
    values[BACK] = acc[0, :, HEAD_DIM:].astype(jnp.bfloat16)
    kv_copies = [
        remote(
            table.at[BACK],
            table.at[BACK - step],
            kv_send.at[at, step - 1],
            kv_recv.at[at, step - 1],
            **holder(rows_at + step),
        )
        for step in range(1, BACK + 1)
        for at, table in enumerate((keys, values))
    ]
    go(kv_copies)
    project((1, 3), 2, 1)
    w_wait(4)
    project((4, 1), 0, 1)
    project((4, 1), 1, 2)
    project((4, 1), 2, 1)
    arrive(kv_copies)

    def attend(chunk, head):
        columns_here = pl.ds(pl.multiple_of(head * HEAD_DIM, HEAD_DIM), HEAD_DIM)
        tile = 256
        tiles = range(ROWS // tile)
        spans = [slice(r * tile, (r + 1) * tile) for r in tiles]
        query = [acc[chunk, spans[r], columns_here].astype(jnp.bfloat16) for r in tiles]
        run_max = [jnp.full((tile, 1), NEG_FLOOR, jnp.float32) for r in tiles]
        sums = [jnp.zeros((tile, 128), jnp.float32) for r in tiles]
        output = [jnp.zeros((tile, HEAD_DIM), jnp.float32) for r in tiles]
        for j in range(BACK + 1):
            for r in tiles:
                low = r * tile if j == 0 else 0
                high = (r + 1) * tile if j == BACK else STEP
                scores = jnp.dot(
                    query[r], keys[j, :, low:high], preferred_element_type=jnp.float32
                )
                scores = scores * SCALING + bias[j, spans[r], low:high]
                new_max = jnp.maximum(run_max[r], jnp.max(scores, axis=-1, keepdims=True))
                rescale = jnp.exp2(run_max[r] - new_max)
                probs = jnp.exp2(scores - new_max)
                output[r] = output[r] * rescale + jnp.dot(
                    probs.astype(jnp.bfloat16),
                    values[j, low:high, :],
                    preferred_element_type=jnp.float32,
                )
                partial = probs[:, :128]
                for first in range(128, high - low, 128):
                    partial = partial + probs[:, first : first + 128]
                sums[r] = sums[r] * rescale + partial
                run_max[r] = new_max
        for r in tiles:
            total = jnp.sum(sums[r], axis=-1, keepdims=True)
            attended[spans[r], columns_here] = (output[r] / total).astype(jnp.bfloat16)

    own_rows = pl.ds(pl.multiple_of(rows_at * BLOCK, BLOCK), BLOCK)

    def slot_copy(at, span, index, step):
        target = (rows_at + step) % LAYERS
        return remote(
            slots.at[at, pl.ds(pl.multiple_of(target * BLOCK, BLOCK), BLOCK), span],
            landed.at[at, own_rows, span],
            s_send.at[index, step],
            s_recv.at[index, step],
            layer=target,
            attn=group,
        )

    def slot_send(at, first, width, index):
        span = pl.ds(first, width)
        slots[at, :, span] = jnp.dot(
            pick[...], attended[:, span], preferred_element_type=jnp.float32
        ).astype(jnp.bfloat16)
        for step in range(1, LAYERS):
            slot_copy(at, span, index, step).start()
        own = slot_copy(at, span, index, 0)

        @pl.when(away)
        def _():
            own.start()

        @pl.when(home)
        def _():
            landed[at, own_rows, span] = slots[at, own_rows, span]

    def slot_take(at, first, width, index, column):
        span = pl.ds(first, width)
        for step in range(1, LAYERS):
            slot_copy(at, span, index, step).wait()
        own = slot_copy(at, span, index, 0)

        @pl.when(away)
        def _():
            own.wait()

        out_ref[:, pl.ds(column, width)] = jnp.dot(
            keep[...], landed[at, :, span], preferred_element_type=jnp.float32
        ).astype(jnp.bfloat16)

    @pl.loop(0, CHUNKS - 2)
    def _(at):
        @pl.loop(0, 2)
        def _(head):
            attend(at + 1, head)

        slot_send(at, 0, WIDE, at)

        @pl.when(at > 0)
        def _():
            slot_take(at - 1, 0, WIDE, at - 1, pl.multiple_of((at - 1) * WIDE, WIDE))

    last = CHUNKS - 2
    for head in range(2):
        attend(last + 1, head)
        slot_send(last, head * HEAD_DIM, HEAD_DIM, last + head)
        if head == 0:
            slot_take(last - 1, 0, WIDE, last - 1, (last - 1) * WIDE)
    for head in range(2):
        slot_take(
            last, head * HEAD_DIM, HEAD_DIM, last + head, last * WIDE + head * HEAD_DIM
        )

    for who, copies in sent.items():

        def done(copies=copies):
            for copy in copies:
                copy.wait_send()

        if who == "all":
            done()
        else:
            pl.when(condition[who])(done)


def fused(tokens, gain, weight, docs, plan):
    vmem = pl.BlockSpec(memory_space=pltpu.VMEM)
    dma = pltpu.SemaphoreType.DMA
    bf16, f32 = jnp.bfloat16, jnp.float32
    return pl.pallas_call(
        fused_kernel,
        out_shape=jax.ShapeDtypeStruct((ROWS, GROUP * HEAD_DIM), bf16),
        in_specs=[
            vmem,
            vmem,
            pl.BlockSpec(memory_space=pl.ANY),
            vmem,
            pl.BlockSpec(memory_space=pltpu.SMEM),
        ],
        out_specs=vmem,
        scratch_shapes=[
            pltpu.VMEM((ROWS, COLS), bf16),
            pltpu.VMEM((ATTN, ROWS, COLS), bf16),
            pltpu.VMEM((CHUNKS, 2, RING, 2, 2, HALF, WIDE), bf16),
            pltpu.VMEM((BACK + 1, HEAD_DIM, STEP), bf16),
            pltpu.VMEM((BACK + 1, STEP, HEAD_DIM), bf16),
            pltpu.VMEM((BACK + 1, ROWS, STEP), f32),
            pltpu.VMEM((LAYERS * BLOCK, ROWS), bf16),
            pltpu.VMEM((ROWS, LAYERS * BLOCK), bf16),
            pltpu.VMEM((ROWS, WIDE), bf16),
            pltpu.VMEM((CHUNKS - 1, LAYERS * BLOCK, WIDE), bf16),
            pltpu.VMEM((CHUNKS - 1, LAYERS * BLOCK, WIDE), bf16),
            pltpu.VMEM((CHUNKS, ROWS, WIDE), f32),
            pltpu.VMEM((ATTN, 8, ROWS), f32),
            dma((CHUNKS,)),
            dma((CHUNKS, 2)),
            dma((CHUNKS, 2)),
            dma((CHUNKS, 8)),
            dma((CHUNKS, 8)),
            dma((CHUNKS, 4)),
            dma((CHUNKS, 4)),
            dma((2, 2)),
            dma((2, 2)),
            dma((6,)),
            dma((6,)),
            dma((ATTN - 1,)),
            dma((ATTN - 1,)),
            dma((2, BACK)),
            dma((2, BACK)),
            dma((CHUNKS, LAYERS)),
            dma((CHUNKS, LAYERS)),
        ],
        compiler_params=pltpu.CompilerParams(
            collective_id=0, has_side_effects=True, vmem_limit_bytes=60 * 2**20
        ),
        cost_estimate=pl.CostEstimate(
            flops=2 * ROWS * 8192 * 1280, bytes_accessed=30 * 2**20, transcendentals=10 * 2**20
        ),
    )(tokens, gain, weight, docs, plan)


def solution(mesh):
    placed = (P("layer", "attn"), P(), P("layer", "attn"), P(), P())
    return jax.shard_map(
        fused, mesh=mesh, in_specs=placed, out_specs=P("layer", "attn"), check_vma=False
    )
```
